32 devices in a mesh: band: 4 (over x, core), facet: 8 (over z, y).
Axes of the slice: x: 2, y: 2, z: 4, core: 2. Of those that a mesh axis runs over, the one named last changes fastest.
Arguments:
- coeffs: float32 [4, 8, 256, 256], P('band', 'facet'), may hold values from -6 to 6
- dirty: float32 [16, 8, 256, 256], P('band', 'facet'), may hold values from -6 to 6
- psf: float32 [16, 8, 129, 129], P('band', 'facet'), may hold values from -0.046875 to 0.046875
- band_offset: float32 [16], P('band'), may hold values from -0.5 to 0.5
Outputs:
- gradient: float32 [4, 8, 256, 256], P('band', 'facet')
The draws below stay inside these ranges and needn't reach their ends.
All inputs are finite; a program needn't handle non-finite values.
Results may differ from the reference program's by a relative error of at most 0.0003.
Values sent between devices are 32-bit elements; how exact they have to be, the bound alone decides.
A program may use at most 64 MiB of HBM per device.

```python
import jax
import jax.numpy as jnp
from jax import lax

P_SIZE = 256
B = 64
L = 512
BANDS = 16
TERMS = 4
FGY = 4
K = 129
FACETS = 8
FROWS = 2


def block_levels(stream_key, shape, pieces, smallest, high):
    gain, own = 1.0, jax.random.fold_in(stream_key, 6)
    for dim, parts in pieces:
        heights = jnp.exp(jax.random.uniform(jax.random.fold_in(own, dim), (parts,), jnp.float32, smallest / len(pieces), high / len(pieces)))
        gain = gain * jnp.repeat(heights, shape[dim] // parts).reshape([-1 if axis == dim else 1 for axis in range(len(shape))])
    return gain


def centred(rng, shape, spread, reach, shards=(), kind=jnp.bfloat16):
    array = jax.random.normal(rng, shape, jnp.float32) * spread
    if len(shards) > 0:
        array = block_levels(rng, shape, shards, -0.22, 0.18) * array
    return jnp.clip(array, min=-reach, max=reach).astype(kind)


def setup_inputs(seed: int = 0) -> dict:
    arg_keys = jax.random.split(jax.random.key(seed), 5)
    return {
        "coeffs": centred(arg_keys[0], (TERMS, FACETS, P_SIZE, P_SIZE), 1.0, 6.0, ((0, 4), (1, 8)), jnp.float32),
        "dirty": centred(arg_keys[1], (BANDS, FACETS, P_SIZE, P_SIZE), 1.0, 6.0, ((0, 4), (1, 8)), jnp.float32),
        "psf": centred(arg_keys[2], (BANDS, FACETS, K, K), (K * K) ** -0.5, 0.046875, ((0, 4), (1, 8)), jnp.float32),
        "band_offset": jnp.clip(jax.random.uniform(arg_keys[3], (BANDS,), jnp.float32, -0.5, 0.5) * block_levels(arg_keys[3], (BANDS,), ((0, 4),), -0.4, 0.0), -0.5, 0.5),
    }


def band_weights(band_offset):
    columns = [jnp.ones_like(band_offset)]
    for power in range(1, TERMS):
        columns.append(columns[-1] * band_offset)
    return jnp.stack(columns, axis=1)


def reference(coeffs, dirty, psf, band_offset):
    weights = band_weights(band_offset)
    span = P_SIZE + 2 * B
    offset = FGY + FGY // 2
    position = ((jnp.arange(FACETS) + offset) % FACETS).astype(jnp.int32)
    rows_idx = (position // FGY).astype(jnp.int32)
    cols_idx = (position % FGY).astype(jnp.int32)

    def one_band(carry, inputs):
        weight_row, dirty_band, psf_band = inputs
        model = jnp.einsum("t,tfij->fij", weight_row, coeffs, precision=lax.Precision.HIGHEST)
        placed = jnp.roll(model, offset, axis=0)
        sky = placed.reshape(FROWS, FGY, P_SIZE, P_SIZE).transpose(0, 2, 1, 3).reshape(FROWS * P_SIZE, FGY * P_SIZE)
        padded = jnp.pad(sky, B)

        def window(row, col):
            return lax.dynamic_slice(padded, ((row * P_SIZE).astype(jnp.int32), (col * P_SIZE).astype(jnp.int32)), (span, span))

        extended = jax.vmap(window)(rows_idx, cols_idx)
        ext_pad = jnp.pad(extended, ((0, 0), (0, L - span), (0, L - span)))
        kernel = jnp.pad(psf_band, ((0, 0), (0, L - K), (0, L - K)))
        kernel = jnp.roll(kernel, (-B, -B), axis=(1, 2))
        spectrum = jnp.fft.rfft2(ext_pad) * jnp.fft.rfft2(kernel)
        conv = jnp.fft.irfft2(spectrum, s=(L, L))
        smeared = conv[:, B:B + P_SIZE, B:B + P_SIZE].astype(carry.dtype)
        residual = dirty_band - smeared
        carry = carry + weight_row[:, None, None, None] * residual[None]
        return carry, None

    start = jnp.zeros((TERMS, FACETS, P_SIZE, P_SIZE), jnp.float32)
    gradient, unused = lax.scan(one_band, start, (weights, dirty, psf))
    return gradient
```

```python
import numpy as np
import jax
import jax.numpy as jnp
from jax import lax
from jax.sharding import PartitionSpec as P

B = 64
TERMS = 4
FGY = 4
HIGH = lax.Precision.HIGH


def padded(array, sides, width):
    for axis, dim in sides:
        peers, length = (lax.axis_size(axis), array.shape[dim])
        up = [(i, (i + 1) % peers) for i in range(peers)]
        down = [(j, i) for i, j in up]
        last = lax.slice_in_dim(array, length - width, length, axis=dim)
        initial = lax.slice_in_dim(array, 0, width, axis=dim)
        before = lax.ppermute(last, axis, up)
        after = lax.ppermute(initial, axis, down)
        array = jnp.concatenate([before, array, after], axis=dim)
    return array


def shifted(array, axis, by):
    peers = lax.axis_size(axis)
    return lax.ppermute(array, axis, [(i, (i + by) % peers) for i in range(peers)])


def extend(field, column, row_of):
    inner = field.shape[1]
    wide = padded(field, (("facet", 2),), B)
    positions = jnp.arange(inner + 2 * B)
    keep_left = column > 0
    keep_right = column < FGY - 1
    keep = jnp.where(positions < B, keep_left, jnp.where(positions >= B + inner, keep_right, True))
    wide = jnp.where(keep[None, None, :], wide, 0.0)
    above = shifted(wide[:, inner - B :, :], "facet", FGY)
    below = shifted(wide[:, :B, :], "facet", -FGY)
    above = jnp.where(row_of > 0, above, 0.0)
    below = jnp.where(row_of < lax.axis_size("facet") // FGY - 1, below, 0.0)
    return jnp.concatenate([above, wide, below], axis=1)


def forward_table(positions, length, half):
    k = np.arange(half)
    angle = 2 * np.pi * ((k[:, None] * positions[None, :]) % length) / length
    ok = (k <= length // 2)[:, None]
    return np.concatenate([np.cos(angle) * ok, np.sin(angle) * ok], axis=0)


def inverse_table(positions, length, half):
    k = np.arange(half)
    fold = np.where((k == 0) | (k == length // 2), 1.0, 2.0) / length
    return forward_table(positions, length, half) * np.concatenate([fold, fold])[:, None]


def powers(band_offset, count):
    columns = [jnp.ones_like(band_offset)]
    for _ in range(1, count):
        columns.append(columns[-1] * band_offset)
    return jnp.stack(columns, axis=1)


def dot(a, b):
    return jnp.matmul(a, b, precision=HIGH)


def halves(x, hr, hc):
    cc, cs = x[..., :hr, :hc], x[..., :hr, hc:]
    sc, ss = x[..., hr:, :hc], x[..., hr:, hc:]
    return (cc - ss, sc + cs, cc + ss, sc - cs)


def body(coeffs, dirty, psf, band_offset):
    size = coeffs.shape[-1]
    span = size + 2 * B
    k = psf.shape[-1]
    hr, hc = 200, 256
    pos = np.arange(span) - B
    ker = np.arange(k) - B
    out = np.arange(size)
    f32 = lambda a: jnp.asarray(a.astype(np.float32))
    ar, ac = f32(forward_table(pos, span, hr)), f32(forward_table(pos, span, hc).T)
    pr, pc = f32(forward_table(ker, span, hr)), f32(forward_table(ker, span, hc).T)
    br, bc = f32(inverse_table(out, span, hr).T / 2), f32(inverse_table(out, span, hc))

    facets = lax.axis_size("facet")
    position = (lax.axis_index("facet") + FGY + FGY // 2) % facets
    window = extend(coeffs[:, 0], position % FGY, position // FGY)[0]
    weights = powers(band_offset, 2 * TERMS - 1)
    combos = jnp.einsum("bs,bij->sij", weights, psf[:, 0], precision=HIGH)
    combos = lax.psum(combos, "band")
    mine = lax.dynamic_slice_in_dim(combos, lax.axis_index("band"), TERMS, axis=0)
    field = dot(ar, dot(window, ac))
    kern = dot(pr, dot(mine, pc))
    a, b, c, d = halves(field, hr, hc)
    e, f, g, h = halves(kern, hr, hc)
    re1, im1 = a * e - b * f, a * f + b * e
    re2, im2 = c * g - d * h, c * h + d * g
    z = jnp.concatenate(
        [
            jnp.concatenate([re1 + re2, im1 - im2], axis=2),
            jnp.concatenate([im1 + im2, re2 - re1], axis=2),
        ],
        axis=1,
    )
    smeared = dot(dot(br, z), bc)
    partial = jnp.einsum("bt,bij->tij", weights[:, :TERMS], dirty[:, 0], precision=HIGH) - smeared
    share = lax.psum_scatter(partial, "band", scatter_dimension=0, tiled=True)
    return share[:, None]


def solution(mesh):
    placed = (
        P("band", "facet", None, None),
        P("band", "facet", None, None),
        P("band", "facet", None, None),
        P("band"),
    )
    return jax.shard_map(
        body, mesh=mesh, in_specs=placed, out_specs=P("band", "facet", None, None), check_vma=False
    )
```

```python
import ml_dtypes
import numpy as np
import jax
import jax.numpy as jnp
from jax import lax
from jax.experimental import pallas as pl
from jax.experimental.pallas import tpu as pltpu
from jax.sharding import PartitionSpec as P

B = 64
TERMS = 4
FGY = 4
POWERS = 2 * TERMS - 1
HR = 208
HC = 256
KROWS = 144
LANES = 128
F32 = jnp.float32
BF16 = jnp.bfloat16
NEIGHBOURS = [(dr, dc) for dr in (-1, 0, 1) for dc in (-1, 0, 1) if (dr, dc) != (0, 0)]


def forward_table(positions, length, half):
    k = np.arange(half)
    angle = 2 * np.pi * ((k[:, None] * positions[None, :]) % length) / length
    ok = (k <= length // 2)[:, None]
    return np.concatenate([np.cos(angle) * ok, np.sin(angle) * ok], axis=0)


def inverse_table(positions, length, half):
    k = np.arange(half)
    fold = np.where((k == 0) | (k == length // 2), 1.0, 2.0) / length
    return forward_table(positions, length, half) * np.concatenate([fold, fold])[:, None]


def split_table(table):
    hi = table.astype(np.float32).astype(ml_dtypes.bfloat16)
    lo = (table - hi.astype(np.float64)).astype(np.float32).astype(ml_dtypes.bfloat16)
    return hi, lo


def left_table(table, width):
    hi, lo = split_table(table)
    whole = np.concatenate([hi, hi, lo], axis=1)
    return np.pad(whole, ((0, 0), (0, width - whole.shape[1])))


def right_table(table):
    hi, lo = split_table(table)
    return np.concatenate([hi, lo, hi], axis=0)


def tables(size, span, k):
    pos = np.arange(span)
    out = np.arange(size)
    ker = np.arange(k) - B
    field_cols = right_table(forward_table(pos, span, HC).T)
    field_rows = left_table(forward_table(pos, span, HR), 3 * span)
    kern = forward_table(ker, span, HC).T
    kern = np.concatenate([kern[:LANES], np.repeat(kern[LANES:], LANES, axis=0)], axis=0)
    kern_cols = right_table(kern)
    rows = np.pad(forward_table(ker, span, HR), ((0, 0), (0, KROWS - k)))
    kern_rows = left_table(rows, 512)
    back_rows = left_table(inverse_table(out, span, HR).T / 2, 1280)
    back_cols = right_table(inverse_table(out, span, HC))
    return field_cols, field_rows, kern_cols, kern_rows, back_rows, back_cols


def split(x):
    hi = x.astype(BF16)
    return hi, (x - hi.astype(F32)).astype(BF16)


def put_left(ref, x, rows):
    hi, lo = split(x)
    w = x.shape[1]
    ref[rows, 0:w] = hi
    ref[rows, w : 2 * w] = hi
    ref[rows, 2 * w : 3 * w] = lo


def put_right(ref, x, at=0, pitch=None):
    hi, lo = split(x)
    h = x.shape[0]
    pitch = pitch or h
    ref[at : at + h] = hi
    ref[pitch + at : pitch + at + h] = lo
    ref[2 * pitch + at : 2 * pitch + at + h] = hi


def dot(a, b):
    return jnp.dot(a, b, preferred_element_type=F32)


def half_mask(shape):
    return lax.broadcasted_iota(jnp.int32, shape, 1) < LANES // 2


def pack(first, second, left):
    mask = half_mask(first.shape)
    moved = pltpu.roll(second, LANES // 2, 1)
    return jnp.where(mask, first, moved) if left else jnp.where(mask, moved, first)


def kernel(
    facets, size, bands,
    coeffs, dirty_hbm, psf, offset, *refs,
):
    tables_hbm = refs[:6]
    out = refs[6]
    (fc, fr, kc, kr, br, bc, dirty, local_sem,
     comb, recv_a, recv_b, fsum, xrecv, side, side_in, corner, corner_in, vert_in,
     xl, yr, pleft, kright, zright, wleft, field, kern, part, pair_in, term_x, term_in,
     halo_send, halo_recv, s_send, s_recv, x_send, x_recv, f_send, f_recv,
     t_send, t_recv) = refs[7:]
    span = size + 2 * B
    vm = (fc, fr, kc, kr, br, bc)

    g = lax.axis_index("band")
    facet = lax.axis_index("facet")
    chip, core = g // 2, g % 2
    sib = {"band": 2 * chip + 1 - core}
    far = {"band": 2 * (1 - chip) + core}
    q = (facet + FGY + FGY // 2) % facets
    row, col = q // FGY, q % FGY

    local = [pltpu.make_async_copy(tables_hbm[i], vm[i], local_sem.at[i]) for i in range(6)]
    local.append(pltpu.make_async_copy(dirty_hbm, dirty, local_sem.at[6]))
    for copy in local:
        copy.start()

    def exists(d):
        r, c = row + d[0], col + d[1]
        return (r >= 0) & (r < facets // FGY) & (c >= 0) & (c < FGY)

    def device(d):
        return {"facet": (facet + FGY * d[0] + d[1] + facets) % facets}

    barrier = pltpu.get_barrier_semaphore()
    count = 2
    for d in NEIGHBOURS:
        there = exists(d)
        count = count + there.astype(jnp.int32)

        @pl.when(there)
        def _():
            pl.semaphore_signal(barrier, inc=1, device_id=device(d))

    for peer in (sib, far):
        pl.semaphore_signal(barrier, inc=1, device_id=peer)

    powers = []
    for b in range(bands):
        w = offset[b]
        row_b = [jnp.float32(1.0)]
        for _ in range(1, POWERS):
            row_b.append(row_b[-1] * w)
        powers.append(row_b)

    k = psf.shape[-1]
    late = chip == 1

    def place(s):
        return s + jnp.where(late & (s >= 5), 1, 0)

    last = jnp.where(late, 5, 7)
    lane = lax.broadcasted_iota(jnp.int32, (1, LANES), 1)
    comb[:, LANES:KROWS, :] = jnp.zeros((8, KROWS - LANES, LANES), F32)
    for s in range(POWERS):
        total = psf[0, 0, :, 0:LANES]
        if s:
            total = total * powers[0][s]
        for b in range(1, bands):
            total += psf[b, 0, :, 0:LANES] * powers[b][s]
        comb[place(jnp.int32(s)), 0:k, :] = total
    total = jnp.zeros((k, LANES), F32)
    for b in range(bands):
        w_row = jnp.zeros((1, LANES), F32)
        for s in range(POWERS):
            w_row = jnp.where(lane == s, powers[b][s], w_row)
        total += psf[b, 0, :, LANES:k] * w_row
    comb[last, 0:k, :] = total

    h = size // 2
    side[0] = pack(coeffs[0, 0, 0:h, 0:LANES], coeffs[0, 0, h:size, 0:LANES], True)
    side[1] = pack(
        coeffs[0, 0, 0:h, size - LANES : size], coeffs[0, 0, h:size, size - LANES : size], False
    )
    for i, top in enumerate((0, size - B)):
        for j in range(2):
            lanes = slice(0, LANES) if j == 0 else slice(size - LANES, size)
            corner[2 * i + j] = pack(
                coeffs[0, 0, top : top + B // 2, lanes],
                coeffs[0, 0, top + B // 2 : top + B, lanes],
                j == 0,
            )

    def halo(d):
        dr, dc = d
        if dr == 0:
            i = (dc + 1) // 2
            src, dst = side.at[i], side_in.at[i]
        elif dc == 0:
            i = (dr + 1) // 2
            src = coeffs.at[0, 0, pl.ds(i * (size - B), B), :]
            dst = vert_in.at[i]
        else:
            i = (dr + 1) + (dc + 1) // 2
            src, dst = corner.at[i], corner_in.at[i]
        n = NEIGHBOURS.index(d)
        return pltpu.make_async_remote_copy(
            src, dst, halo_send.at[n], halo_recv.at[n], device_id=device(d)
        )

    pl.semaphore_wait(barrier, count)

    def start_of(c, who):
        return 2 * (1 - who) + 3 * c

    a_copy = pltpu.make_async_remote_copy(
        comb.at[pl.ds(start_of(1 - core, chip), 3)], recv_a, s_send.at[0], s_recv.at[0], device_id=sib
    )
    a_copy.start()
    order = sorted(NEIGHBOURS, key=lambda d: abs(d[0]) + abs(d[1]) == 2)
    for d in order:
        @pl.when(exists(d))
        def _():
            halo(d).start()

    b_copy = pltpu.make_async_remote_copy(comb, recv_b, s_send.at[1], s_recv.at[1], device_id=sib)
    b_copy.start()

    a_copy.wait_recv()
    mine = start_of(core, chip)
    x_copies, f_copies = [], []
    for i in range(3):
        fsum[i] = comb[mine + i] + recv_a[i]
        slot = xrecv.at[3 * core + i]
        x_copies.append(
            pltpu.make_async_remote_copy(fsum.at[i], slot, x_send.at[i], x_recv.at[i], device_id=far)
        )
        f_copies.append(
            pltpu.make_async_remote_copy(slot, slot, f_send.at[i], f_recv.at[i], device_id=sib)
        )
        x_copies[i].start()

    for d in NEIGHBOURS:
        dr, dc = d
        there = exists(d)
        incoming = halo((-dr, -dc))

        @pl.when(there)
        def _():
            incoming.wait_recv()

        if dr == 0:
            ref, i = side_in, (1 - dc) // 2
        elif dc == 0:
            ref, i = vert_in, (1 - dr) // 2
        else:
            ref, i = corner_in, (1 - dr) + (1 - dc) // 2

        @pl.when(jnp.logical_not(there))
        def _():
            ref[i] = jnp.zeros(ref.shape[1:], F32)

    for i in range(3):
        x_copies[i].wait_recv()
        f_copies[i].start()

    mask = half_mask((h, LANES))
    small = half_mask((B // 2, LANES))
    local[0].wait()

    def edge(right, left, m):
        top = jnp.where(m, right, left)
        bottom = pltpu.roll(jnp.where(m, left, right), LANES // 2, 1)
        return top, bottom

    def window(rows, centre, strip):
        put_left(xl, jnp.concatenate([centre, strip], axis=1), rows)

    top, bottom = edge(side_in[0], side_in[1], mask)
    window(pl.ds(0, h), coeffs[0, 0, 0:h, :], top)
    window(pl.ds(h, h), coeffs[0, 0, h:size, :], bottom)
    for i in range(2):
        top, bottom = edge(corner_in[2 * i], corner_in[2 * i + 1], small)
        at = size + i * B
        window(pl.ds(at, B), vert_in[i], jnp.concatenate([top, bottom], axis=0))
    put_right(yr, dot(xl[...], fc[...]))
    local[1].wait()
    full = dot(fr[...], yr[...])

    def halves(x, ref):
        cc, cs = x[:HR, :HC], x[:HR, HC:]
        sc, ss = x[HR:, :HC], x[HR:, HC:]
        ref[0] = cc - ss
        ref[1] = sc + cs
        ref[2] = cc + ss
        ref[3] = sc - cs

    halves(full, field)

    for i in range(3):
        other = xrecv.at[3 * (1 - core) + i]
        pltpu.make_async_remote_copy(
            other, other, f_send.at[i], f_recv.at[i], device_id=sib
        ).wait_recv()
    b_copy.wait_recv()
    local[2].wait()
    local[3].wait()
    kright[3 * KROWS : 512] = jnp.zeros((512 - 3 * KROWS, 2 * HC), BF16)
    zright[6 * HR : 1280] = jnp.zeros((1280 - 6 * HR, 2 * HC), BF16)
    column = comb[last] + recv_b[last] + xrecv[5]

    @pl.loop(0, TERMS)
    def _(t):
        s = g + t
        at = place(s)
        main = comb[at] + recv_b[at] + xrecv[core + t]
        own = jnp.where(lane == s, column, 0.0)
        put_left(pleft, jnp.concatenate([main, own], axis=1), slice(0, KROWS))
        put_right(kright, dot(pleft[...], kc[...]))
        halves(dot(kr[...], kright[...]), kern.at[t])

    for copy in local[4:]:
        copy.wait()

    def weight(b, t):
        w = powers[b]
        return jnp.where(t == 0, w[0], jnp.where(t == 1, w[1], jnp.where(t == 2, w[2], w[3])))

    def term(t):
        a, b, c, d = (field[i] for i in range(4))
        e, f, p, r = (kern[t, i] for i in range(4))
        re1, im1 = a * e - b * f, a * f + b * e
        re2, im2 = c * p - d * r, c * r + d * p
        put_right(zright, jnp.concatenate([re1 + re2, im1 - im2], axis=1), 0, 2 * HR)
        put_right(zright, jnp.concatenate([im1 + im2, re2 - re1], axis=1), HR, 2 * HR)
        put_left(wleft, dot(br[...], zright[...]), slice(0, size))
        total = dirty[0, 0] * weight(0, t)
        for n in range(1, bands):
            total += dirty[n, 0] * weight(n, t)
        return total - dot(wleft[...], bc[...])

    def pair_copy(i):
        return pltpu.make_async_remote_copy(
            part.at[i], pair_in.at[i], t_send.at[i], t_recv.at[i], device_id=sib
        )

    away, home = 2 * (1 - chip), 2 * chip
    part[0] = term(away + 1 - core)
    first = pair_copy(0)
    first.start()
    total = term(away + core)
    first.wait_recv()
    term_x[...] = total + pair_in[0]
    cross = pltpu.make_async_remote_copy(
        term_x, term_in, t_send.at[2], t_recv.at[2], device_id=far
    )
    cross.start()
    part[1] = term(home + 1 - core)
    second = pair_copy(1)
    second.start()
    total = term(home + core)
    second.wait_recv()
    total += pair_in[1]
    cross.wait_recv()
    out[0, 0] = total + term_in[...]

    for d in NEIGHBOURS:
        @pl.when(exists(d))
        def _():
            halo(d).wait_send()

    for copy in (a_copy, b_copy, *x_copies, *f_copies, first, second, cross):
        copy.wait_send()


def body(coeffs, dirty, psf, band_offset):
    size = coeffs.shape[-1]
    span = size + 2 * B
    bands = dirty.shape[0]
    facets = lax.axis_size("facet")
    consts = tables(size, span, psf.shape[-1])
    vmem = pl.BlockSpec(memory_space=pltpu.VMEM)
    hbm = pl.BlockSpec(memory_space=pl.ANY)
    dma = lambda n: pltpu.SemaphoreType.DMA((n,))
    scratch = [pltpu.VMEM(c.shape, BF16) for c in consts]
    scratch += [
        pltpu.VMEM(dirty.shape, F32),
        dma(7),
        pltpu.VMEM((8, KROWS, LANES), F32),
        pltpu.VMEM((3, KROWS, LANES), F32),
        pltpu.VMEM((8, KROWS, LANES), F32),
        pltpu.VMEM((3, KROWS, LANES), F32),
        pltpu.VMEM((6, KROWS, LANES), F32),
        pltpu.VMEM((2, size // 2, LANES), F32),
        pltpu.VMEM((2, size // 2, LANES), F32),
        pltpu.VMEM((4, B // 2, LANES), F32),
        pltpu.VMEM((4, B // 2, LANES), F32),
        pltpu.VMEM((2, B, size), F32),
        pltpu.VMEM((span, 3 * span), BF16),
        pltpu.VMEM((3 * span, 2 * HC), BF16),
        pltpu.VMEM((KROWS, 6 * LANES), BF16),
        pltpu.VMEM((512, 2 * HC), BF16),
        pltpu.VMEM((1280, 2 * HC), BF16),
        pltpu.VMEM((size, 6 * HC), BF16),
        pltpu.VMEM((4, HR, HC), F32),
        pltpu.VMEM((TERMS, 4, HR, HC), F32),
        pltpu.VMEM((2, size, size), F32),
        pltpu.VMEM((2, size, size), F32),
        pltpu.VMEM((size, size), F32),
        pltpu.VMEM((size, size), F32),
        dma(8), dma(8), dma(2), dma(2), dma(3), dma(3), dma(3), dma(3), dma(3), dma(3),
    ]

    def run(*args):
        kernel(facets, size, bands, *args)

    return pl.pallas_call(
        run,
        out_shape=jax.ShapeDtypeStruct(coeffs.shape, F32),
        in_specs=[vmem, hbm, vmem, pl.BlockSpec(memory_space=pltpu.SMEM)] + [hbm] * 6,
        out_specs=vmem,
        scratch_shapes=scratch,
        compiler_params=pltpu.CompilerParams(
            collective_id=0, has_side_effects=True, vmem_limit_bytes=56 * 1024 * 1024
        ),
        cost_estimate=pl.CostEstimate(flops=4_000_000_000, bytes_accessed=8_000_000, transcendentals=0),
    )(coeffs, dirty, psf, band_offset, *[jnp.asarray(c) for c in consts])


def solution(mesh):
    placed = (
        P("band", "facet", None, None),
        P("band", "facet", None, None),
        P("band", "facet", None, None),
        P("band"),
    )
    return jax.shard_map(
        body, mesh=mesh, in_specs=placed, out_specs=P("band", "facet", None, None), check_vma=False
    )
```

```python
import ml_dtypes
import numpy as np
import jax
import jax.numpy as jnp
from jax import lax
from jax.experimental import pallas as pl
from jax.experimental.pallas import tpu as pltpu
from jax.sharding import PartitionSpec as P

B = 64
TERMS = 4
FGY = 4
POWERS = 2 * TERMS - 1
ORDER = (2, 3, 4, None, 0, 1, 5, 6)
HR = 208
HC = 256
KROWS = 144
SENT = 136
LANES = 128
F32 = jnp.float32
BF16 = jnp.bfloat16
NEIGHBOURS = [(dr, dc) for dr in (-1, 0, 1) for dc in (-1, 0, 1) if (dr, dc) != (0, 0)]


def forward_table(positions, length, half):
    k = np.arange(half)
    angle = 2 * np.pi * ((k[:, None] * positions[None, :]) % length) / length
    ok = (k <= length // 2)[:, None]
    return np.concatenate([np.cos(angle) * ok, np.sin(angle) * ok], axis=0)


def inverse_table(positions, length, half):
    k = np.arange(half)
    fold = np.where((k == 0) | (k == length // 2), 1.0, 2.0) / length
    return forward_table(positions, length, half) * np.concatenate([fold, fold])[:, None]


def split_table(table):
    hi = table.astype(np.float32).astype(ml_dtypes.bfloat16)
    lo = (table - hi.astype(np.float64)).astype(np.float32).astype(ml_dtypes.bfloat16)
    return hi, lo


def left_table(table, width):
    hi, lo = split_table(table)
    whole = np.concatenate([hi, hi, lo], axis=1)
    return np.pad(whole, ((0, 0), (0, width - whole.shape[1])))


def right_table(table):
    hi, lo = split_table(table)
    return np.concatenate([hi, lo, hi], axis=0)


def tables(size, span, k):
    pos = np.arange(span)
    out = np.arange(size)
    ker = np.arange(k) - B
    cols = forward_table(pos, span, HC).T
    field_own, field_edge = right_table(cols[:size]), right_table(cols[size:])
    field_rows = left_table(forward_table(pos, span, HR), 3 * span)
    kern = forward_table(ker, span, HC).T
    kern = np.concatenate([kern[:LANES], np.repeat(kern[LANES:], LANES, axis=0)], axis=0)
    kern_cols = right_table(kern)
    rows = np.pad(forward_table(ker, span, HR), ((0, 0), (0, KROWS - k)))
    kern_rows = left_table(rows, 512)
    back_rows = left_table(inverse_table(out, span, HR).T / 2, 1280)
    back_cols = right_table(inverse_table(out, span, HC))
    return field_own, field_edge, field_rows, kern_cols, kern_rows, back_rows, back_cols


def split(x):
    hi = x.astype(BF16)
    return hi, (x - hi.astype(F32)).astype(BF16)


def put_left(ref, x, row=0):
    hi, lo = split(x)
    h, w = x.shape
    ref[row : row + h, 0:w] = hi
    ref[row : row + h, w : 2 * w] = hi
    ref[row : row + h, 2 * w : 3 * w] = lo


def put_right(ref, x, at=0, pitch=None):
    hi, lo = split(x)
    h = x.shape[0]
    pitch = pitch or h
    ref[at : at + h] = hi
    ref[pitch + at : pitch + at + h] = lo
    ref[2 * pitch + at : 2 * pitch + at + h] = hi


def dot(a, b):
    return jnp.dot(a, b, preferred_element_type=F32)


def half_mask(shape):
    return lax.broadcasted_iota(jnp.int32, shape, 1) < LANES // 2


def pack(first, second, left):
    mask = half_mask(first.shape)
    moved = pltpu.roll(second, LANES // 2, 1)
    return jnp.where(mask, first, moved) if left else jnp.where(mask, moved, first)


def kernel(
    facets, size, bands,
    coeffs, dirty_hbm, psf, offset, *refs,
):
    tables_hbm = refs[:7]
    out, got = refs[7:9]
    (fo, fe, fr, kc, kr, br, bc, dirty, local_sem,
     comb, recv_a, recv_b, fsum, xrecv, side, side_in, corner, corner_in, vert_in,
     xo, xe, own_part, yr, pleft, kright, zright, wleft, field, kern, dsum, part, pair_in, term_x,
     term_in, halo_send, halo_recv, s_send, s_recv, x_send, x_recv, f_send, f_recv,
     t_send, t_recv) = refs[9:]
    vm = (fo, fe, fr, kc, kr, br, bc)

    g = lax.axis_index("band")
    facet = lax.axis_index("facet")
    chip, core = g // 2, g % 2
    sib = {"band": 2 * chip + 1 - core}
    far = {"band": 2 * (1 - chip) + core}
    q = (facet + FGY + FGY // 2) % facets
    row, col = q // FGY, q % FGY

    def exists(d):
        r, c = row + d[0], col + d[1]
        return (r >= 0) & (r < facets // FGY) & (c >= 0) & (c < FGY)

    def device(d):
        return {"facet": (facet + FGY * d[0] + d[1] + facets) % facets}

    barrier = pltpu.get_barrier_semaphore()
    count = 2
    for d in NEIGHBOURS:
        there = exists(d)
        count = count + there.astype(jnp.int32)

        @pl.when(there)
        def _():
            pl.semaphore_signal(barrier, inc=1, device_id=device(d))

    for peer in (sib, far):
        pl.semaphore_signal(barrier, inc=1, device_id=peer)

    local = [pltpu.make_async_copy(dirty_hbm, dirty, local_sem.at[7])]
    local += [pltpu.make_async_copy(tables_hbm[i], vm[i], local_sem.at[i]) for i in range(7)]
    for copy in local:
        copy.start()

    powers = []
    for b in range(bands):
        w = offset[b]
        row_b = [jnp.float32(1.0)]
        for _ in range(1, POWERS):
            row_b.append(row_b[-1] * w)
        powers.append(row_b)

    k = psf.shape[1]
    lane = lax.broadcasted_iota(jnp.int32, (1, LANES), 1)
    comb[:, LANES:SENT, :] = jnp.zeros((8, SENT - LANES, LANES), F32)
    planes = [psf[b, :, 0, 0:LANES] for b in range(bands)]
    for s in range(POWERS):
        total = planes[0]
        if s:
            total = total * powers[0][s]
        for b in range(1, bands):
            total += planes[b] * powers[b][s]
        comb[ORDER.index(s), 0:k, :] = total
    total = jnp.zeros((k, LANES), F32)
    for b in range(bands):
        w_row = jnp.zeros((1, LANES), F32)
        for s in range(POWERS):
            w_row = jnp.where(lane == s, powers[b][s], w_row)
        total += psf[b, :, 0, LANES:k] * w_row
    comb[3, 0:k, :] = total

    h = size // 2
    side[0] = pack(coeffs[0, 0, 0:h, 0:LANES], coeffs[0, 0, h:size, 0:LANES], True)
    side[1] = pack(
        coeffs[0, 0, 0:h, size - LANES : size], coeffs[0, 0, h:size, size - LANES : size], False
    )
    for i, top in enumerate((0, size - B)):
        for j in range(2):
            lanes = slice(0, LANES) if j == 0 else slice(size - LANES, size)
            corner[2 * i + j] = pack(
                coeffs[0, 0, top : top + B // 2, lanes],
                coeffs[0, 0, top + B // 2 : top + B, lanes],
                j == 0,
            )

    def halo(d):
        dr, dc = d
        if dr == 0:
            i = (dc + 1) // 2
            src, dst = side.at[i], side_in.at[i]
        elif dc == 0:
            i = (dr + 1) // 2
            src = coeffs.at[0, 0, pl.ds(i * (size - B), B), :]
            dst = vert_in.at[i]
        else:
            i = (dr + 1) + (dc + 1) // 2
            src, dst = corner.at[i], corner_in.at[i]
        n = NEIGHBOURS.index(d)
        return pltpu.make_async_remote_copy(
            src, dst, halo_send.at[n], halo_recv.at[n], device_id=device(d)
        )

    pl.semaphore_wait(barrier, count)

    def to_sib(src, dst, i):
        return pltpu.make_async_remote_copy(src, dst, s_send.at[i], s_recv.at[i], device_id=sib)

    later = jnp.where(chip == 0, 6, 4)
    a_copies = [to_sib(comb.at[2 * (1 - core) + i], recv_a.at[i], i) for i in range(2)]
    a_copies.append(to_sib(comb.at[later + 1 - core], recv_a.at[2], 2))
    b_copies = [to_sib(comb.at[pl.ds(4 * i, 4)], recv_b.at[pl.ds(4 * i, 4)], 3 + i) for i in range(2)]
    a_copies[0].start()
    a_copies[1].start()
    for d in sorted(NEIGHBOURS, key=lambda d: abs(d[0]) + abs(d[1]) == 2):
        @pl.when(exists(d))
        def _():
            halo(d).start()

    a_copies[2].start()
    b_copies[0].start()
    b_copies[1].start()

    x_copies, f_copies = [], []
    for i in range(3):
        slot = xrecv.at[2 * core + i if i < 2 else 4 + core]
        x_copies.append(
            pltpu.make_async_remote_copy(fsum.at[i], slot, x_send.at[i], x_recv.at[i], device_id=far)
        )
        f_copies.append(
            pltpu.make_async_remote_copy(slot, slot, f_send.at[i], f_recv.at[i], device_id=sib)
        )
        a_copies[i].wait_recv()
        fsum[i] = comb[2 * core + i if i < 2 else later + core] + recv_a[i]
        x_copies[i].start()

    away, home = 2 * (1 - chip), 2 * chip
    terms = (away + 1 - core, away + core, home + 1 - core, home + core)

    def weight(b, t):
        w = powers[b]
        return jnp.where(t == 0, w[0], jnp.where(t == 1, w[1], jnp.where(t == 2, w[2], w[3])))

    kright[:, 3 * KROWS : 512] = jnp.zeros((2, 512 - 3 * KROWS, 2 * HC), BF16)
    zright[6 * HR : 1280] = jnp.zeros((1280 - 6 * HR, 2 * HC), BF16)
    put_left(xo, coeffs[0, 0])
    local[1].wait()
    own_part[...] = dot(xo[0:size], fo[...])
    local[0].wait()
    for i, t in enumerate(terms):
        total = dirty[0, 0] * weight(0, t)
        for n in range(1, bands):
            total += dirty[n, 0] * weight(n, t)
        dsum[i] = total

    for copy in local[2:]:
        copy.wait()

    for i in range(2):
        x_copies[i].wait_recv()
        f_copies[i].start()

    for d in NEIGHBOURS:
        dr, dc = d
        there = exists(d)
        incoming = halo((-dr, -dc))

        @pl.when(there)
        def _():
            incoming.wait_recv()

        if dr == 0:
            ref, i = side_in, (1 - dc) // 2
        elif dc == 0:
            ref, i = vert_in, (1 - dr) // 2
        else:
            ref, i = corner_in, (1 - dr) + (1 - dc) // 2

        @pl.when(jnp.logical_not(there))
        def _():
            ref[i] = jnp.zeros(ref.shape[1:], F32)

    def edge(right, left, m):
        top = jnp.where(m, right, left)
        bottom = pltpu.roll(jnp.where(m, left, right), LANES // 2, 1)
        return jnp.concatenate([top, bottom], axis=0)

    put_left(xe, edge(side_in[0], side_in[1], half_mask((h, LANES))))
    small = half_mask((B // 2, LANES))
    for i in range(2):
        put_left(xo, vert_in[i], size + i * B)
        put_left(xe, edge(corner_in[2 * i], corner_in[2 * i + 1], small), size + i * B)
    total_rows = size + 2 * B
    put_right(yr, own_part[...] + dot(xe[0:size], fe[...]), 0, total_rows)
    put_right(yr, dot(xo[size:], fo[...]) + dot(xe[size:], fe[...]), size, total_rows)
    full = dot(fr[...], yr[...])

    def halves(x, ref):
        cc, cs = x[:HR, :HC], x[:HR, HC:]
        sc, ss = x[HR:, :HC], x[HR:, HC:]
        ref[0] = cc - ss
        ref[1] = sc + cs
        ref[2] = cc + ss
        ref[3] = sc - cs

    halves(full, field)

    def forwarded(i):
        other = xrecv.at[2 * (1 - core) + i if i < 2 else 5 - core]
        pltpu.make_async_remote_copy(
            other, other, f_send.at[i], f_recv.at[i], device_id=sib
        ).wait_recv()

    blank = jnp.zeros((KROWS - SENT, 2 * LANES), F32)

    def kernels(first):
        column = comb[3] + recv_b[3] + xrecv[3]
        for i in range(2):
            s = g + terms[first + i]
            at = jnp.where(s < 2, s + 4, jnp.where(s < 5, s - 2, s + 1))
            slot = jnp.where(s < 2, s + 4, jnp.where(s < 5, s - 2, s - 1))
            main = comb[at] + recv_b[at] + xrecv[slot]
            last = jnp.where(lane == s, column, 0.0)
            block = jnp.concatenate([main, last], axis=1)
            put_left(pleft, jnp.concatenate([block, blank], axis=0), i * KROWS)
        both = dot(pleft[...], kc[...])
        for i in range(2):
            put_right(kright.at[i], both[i * KROWS : (i + 1) * KROWS])
            halves(dot(kr[...], kright[i]), kern.at[i])

    def term(i, put):
        a, b, c, d = (field[n] for n in range(4))
        e, f, p, r = (kern[i % 2, n] for n in range(4))
        re1, im1 = a * e - b * f, a * f + b * e
        re2, im2 = c * p - d * r, c * r + d * p
        put_right(zright, jnp.concatenate([re1 + re2, im1 - im2], axis=1), 0, 2 * HR)
        put_right(zright, jnp.concatenate([im1 + im2, re2 - re1], axis=1), HR, 2 * HR)
        put_left(wleft, dot(br[...], zright[...]))
        for j in range(2):
            rows = slice(j * h, (j + 1) * h)
            put(j, rows, dsum[i, rows] - dot(wleft[rows], bc[...]))

    def pair_copy(i, j):
        n = 2 * i + j
        rows = pl.ds(j * h, h)
        return pltpu.make_async_remote_copy(
            part.at[i, rows], pair_in.at[i, rows], t_send.at[n], t_recv.at[n], device_id=sib
        )

    def cross_copy(j):
        rows = pl.ds(j * h, h)
        return pltpu.make_async_remote_copy(
            term_x.at[rows], term_in.at[rows], t_send.at[4 + j], t_recv.at[4 + j], device_id=far
        )

    pairs = [[pair_copy(i, j) for j in range(2)] for i in range(2)]
    crosses = [cross_copy(j) for j in range(2)]

    def to_pair(i):
        def put(j, rows, value):
            part[i, rows] = value
            pairs[i][j].start()

        return put

    def to_far(j, rows, value):
        pairs[0][j].wait_recv()
        term_x[rows] = value + pair_in[0, rows]
        crosses[j].start()

    def to_out(j, rows, value):
        pairs[1][j].wait_recv()
        out[0, 0, rows] = value + pair_in[1, rows]

    forwarded(0)
    forwarded(1)
    b_copies[0].wait_recv()
    kernels(0)
    x_copies[2].wait_recv()
    f_copies[2].start()
    term(0, to_pair(0))
    term(1, to_far)
    forwarded(2)
    b_copies[1].wait_recv()
    kernels(2)
    term(2, to_pair(1))
    term(3, to_out)
    for j in range(2):
        rows = slice(j * h, (j + 1) * h)
        crosses[j].wait_recv()
        got[0, 0, rows] = term_in[rows]

    for d in NEIGHBOURS:
        @pl.when(exists(d))
        def _():
            halo(d).wait_send()

    for copy in (*a_copies, *b_copies, *x_copies, *f_copies, *pairs[0], *pairs[1], *crosses):
        copy.wait_send()


def body(coeffs, dirty, psf, band_offset):
    size = coeffs.shape[-1]
    span = size + 2 * B
    bands = dirty.shape[0]
    facets = lax.axis_size("facet")
    consts = tables(size, span, psf.shape[-1])
    vmem = pl.BlockSpec(memory_space=pltpu.VMEM)
    hbm = pl.BlockSpec(memory_space=pl.ANY)
    dma = lambda n: pltpu.SemaphoreType.DMA((n,))
    scratch = [pltpu.VMEM(c.shape, BF16) for c in consts]
    scratch += [
        pltpu.VMEM(dirty.shape, F32),
        dma(8),
        pltpu.VMEM((8, SENT, LANES), F32),
        pltpu.VMEM((3, SENT, LANES), F32),
        pltpu.VMEM((8, SENT, LANES), F32),
        pltpu.VMEM((3, SENT, LANES), F32),
        pltpu.VMEM((6, SENT, LANES), F32),
        pltpu.VMEM((2, size // 2, LANES), F32),
        pltpu.VMEM((2, size // 2, LANES), F32),
        pltpu.VMEM((4, B // 2, LANES), F32),
        pltpu.VMEM((4, B // 2, LANES), F32),
        pltpu.VMEM((2, B, size), F32),
        pltpu.VMEM((span, 3 * size), BF16),
        pltpu.VMEM((span, 3 * LANES), BF16),
        pltpu.VMEM((size, 2 * HC), F32),
        pltpu.VMEM((3 * span, 2 * HC), BF16),
        pltpu.VMEM((2 * KROWS, 6 * LANES), BF16),
        pltpu.VMEM((2, 512, 2 * HC), BF16),
        pltpu.VMEM((1280, 2 * HC), BF16),
        pltpu.VMEM((size, 6 * HC), BF16),
        pltpu.VMEM((4, HR, HC), F32),
        pltpu.VMEM((2, 4, HR, HC), F32),
        pltpu.VMEM((TERMS, size, size), F32),
        pltpu.VMEM((2, size, size), F32),
        pltpu.VMEM((2, size, size), F32),
        pltpu.VMEM((size, size), F32),
        pltpu.VMEM((size, size), F32),
        dma(8), dma(8), dma(5), dma(5), dma(3), dma(3), dma(3), dma(3), dma(6), dma(6),
    ]

    def run(*args):
        kernel(facets, size, bands, *args)

    shape = jax.ShapeDtypeStruct(coeffs.shape, F32)
    kept, received = pl.pallas_call(
        run,
        out_shape=(shape, shape),
        in_specs=[vmem, hbm, vmem, pl.BlockSpec(memory_space=pltpu.SMEM)] + [hbm] * 7,
        out_specs=(vmem, vmem),
        scratch_shapes=scratch,
        compiler_params=pltpu.CompilerParams(
            collective_id=0, has_side_effects=True, vmem_limit_bytes=56 * 1024 * 1024
        ),
        cost_estimate=pl.CostEstimate(flops=4_000_000_000, bytes_accessed=8_000_000, transcendentals=0),
    )(coeffs, dirty, psf.transpose(0, 2, 1, 3), band_offset, *[jnp.asarray(c) for c in consts])
    return kept + received


def solution(mesh):
    placed = (
        P("band", "facet", None, None),
        P("band", "facet", None, None),
        P("band", "facet", None, None),
        P("band"),
    )
    return jax.shard_map(
        body, mesh=mesh, in_specs=placed, out_specs=P("band", "facet", None, None), check_vma=False
    )
```

```python
import ml_dtypes
import numpy as np
import jax
import jax.numpy as jnp
from jax import lax
from jax.experimental import pallas as pl
from jax.experimental.pallas import tpu as pltpu
from jax.sharding import PartitionSpec as P

B = 64
TERMS = 4
FGY = 4
POWERS = 2 * TERMS - 1
ORDER = (2, 3, 4, None, 0, 1, 5, 6)
HR = 208
HC = 256
KROWS = 144
SENT = 136
LANES = 128
F32 = jnp.float32
BF16 = jnp.bfloat16
NEIGHBOURS = [(dr, dc) for dr in (-1, 0, 1) for dc in (-1, 0, 1) if (dr, dc) != (0, 0)]


def forward_table(positions, length, half):
    k = np.arange(half)
    angle = 2 * np.pi * ((k[:, None] * positions[None, :]) % length) / length
    ok = (k <= length // 2)[:, None]
    return np.concatenate([np.cos(angle) * ok, np.sin(angle) * ok], axis=0)


def inverse_table(positions, length, half):
    k = np.arange(half)
    fold = np.where((k == 0) | (k == length // 2), 1.0, 2.0) / length
    return forward_table(positions, length, half) * np.concatenate([fold, fold])[:, None]


def split_table(table):
    hi = table.astype(np.float32).astype(ml_dtypes.bfloat16)
    lo = (table - hi.astype(np.float64)).astype(np.float32).astype(ml_dtypes.bfloat16)
    return hi, lo


def left_table(table, width):
    hi, lo = split_table(table)
    whole = np.concatenate([hi, hi, lo], axis=1)
    return np.pad(whole, ((0, 0), (0, width - whole.shape[1])))


def right_table(table):
    hi, lo = split_table(table)
    return np.concatenate([hi, lo, hi], axis=0)


def tables(size, span, k):
    pos = np.arange(span)
    out = np.arange(size)
    ker = np.arange(k) - B
    cols = forward_table(pos, span, HC).T
    field_own, field_edge = right_table(cols[:size]), right_table(cols[size:])
    field_rows = left_table(forward_table(pos, span, HR), 3 * span)
    kern = forward_table(ker, span, HC).T
    kern = np.concatenate([kern[:LANES], np.repeat(kern[LANES:], LANES, axis=0)], axis=0)
    kern_cols = right_table(kern)
    rows = np.pad(forward_table(ker, span, HR), ((0, 0), (0, KROWS - k)))
    kern_rows = left_table(rows, 512)
    back_rows = left_table(inverse_table(out, span, HR).T / 2, 1280)
    back_cols = right_table(inverse_table(out, span, HC))
    return field_own, field_edge, field_rows, kern_cols, kern_rows, back_rows, back_cols


def split(x):
    hi = x.astype(BF16)
    return hi, (x - hi.astype(F32)).astype(BF16)


def put_left(ref, load, height, row=0, step=16):
    for r in range(0, height, step):
        x = load(slice(r, r + step))
        hi, lo = split(x)
        w = x.shape[1]
        rows = slice(row + r, row + r + step)
        ref[rows, 0:w] = hi
        ref[rows, w : 2 * w] = hi
        ref[rows, 2 * w : 3 * w] = lo


def put_right(ref, load, height, pitch, step=16):
    for r in range(0, height, step):
        hi, lo = split(load(slice(r, r + step)))
        ref[r : r + step] = hi
        ref[pitch + r : pitch + r + step] = lo
        ref[2 * pitch + r : 2 * pitch + r + step] = hi


def dot(a, b):
    return jnp.dot(a, b, preferred_element_type=F32)


def half_mask(shape):
    return lax.broadcasted_iota(jnp.int32, shape, 1) < LANES // 2


def pack(first, second, left):
    mask = half_mask(first.shape)
    moved = pltpu.roll(second, LANES // 2, 1)
    return jnp.where(mask, first, moved) if left else jnp.where(mask, moved, first)


def kernel(
    facets, size, bands,
    coeffs_hbm, dirty_hbm, psf_hbm, offset, *refs,
):
    tables_hbm = refs[:7]
    out, got = refs[7:9]
    (fo, fe, fr, kc, kr, br, bc, coeffs, dirty, psf, acc, kacc, local_sem,
     comb, recv_a, recv_b, fsum, xrecv, side, side_in, corner, corner_in, vert_in,
     xo, xe, own_part, yr, pleft, kright, zright, wleft, field, kern, dsum, part, pair_in, term_x,
     term_in, halo_send, halo_recv, s_send, s_recv, x_send, x_recv, f_send, f_recv,
     t_send, t_recv) = refs[9:]
    vm = (fo, fe, fr, kc, kr, br, bc)

    g = lax.axis_index("band")
    facet = lax.axis_index("facet")
    chip, core = g // 2, g % 2
    sib = {"band": 2 * chip + 1 - core}
    far = {"band": 2 * (1 - chip) + core}
    q = (facet + FGY + FGY // 2) % facets
    row, col = q // FGY, q % FGY

    def exists(d):
        r, c = row + d[0], col + d[1]
        return (r >= 0) & (r < facets // FGY) & (c >= 0) & (c < FGY)

    def device(d):
        return {"facet": (facet + FGY * d[0] + d[1] + facets) % facets}

    inputs = [
        pltpu.make_async_copy(psf_hbm, psf, local_sem.at[8]),
        pltpu.make_async_copy(coeffs_hbm, coeffs, local_sem.at[9]),
    ]
    for copy in inputs:
        copy.start()

    barrier = pltpu.get_barrier_semaphore()
    count = 2
    for d in NEIGHBOURS:
        there = exists(d)
        count = count + there.astype(jnp.int32)

        @pl.when(there)
        def _():
            pl.semaphore_signal(barrier, inc=1, device_id=device(d))

    for peer in (sib, far):
        pl.semaphore_signal(barrier, inc=1, device_id=peer)

    local = [pltpu.make_async_copy(dirty_hbm, dirty, local_sem.at[7])]
    local += [pltpu.make_async_copy(tables_hbm[i], vm[i], local_sem.at[i]) for i in range(7)]
    for copy in local:
        copy.start()

    powers = []
    for b in range(bands):
        w = offset[b]
        row_b = [jnp.float32(1.0)]
        for _ in range(1, POWERS):
            row_b.append(row_b[-1] * w)
        powers.append(row_b)

    k = psf.shape[1]
    lane = lax.broadcasted_iota(jnp.int32, (1, LANES), 1)
    comb[:, LANES:SENT, :] = jnp.zeros((8, SENT - LANES, LANES), F32)
    w_rows = []
    for b in range(bands):
        w_row = jnp.zeros((1, LANES), F32)
        for s in range(POWERS):
            w_row = jnp.where(lane == s, powers[b][s], w_row)
        w_rows.append(w_row)
    inputs[0].wait()
    for top in range(0, k, 32):
        rows = slice(top, min(top + 32, k))
        planes = [psf[b, rows, 0, 0:LANES] for b in range(bands)]
        for s in range(POWERS):
            total = planes[0]
            if s:
                total = total * powers[0][s]
            for b in range(1, bands):
                total += planes[b] * powers[b][s]
            comb[ORDER.index(s), rows, :] = total
        total = psf[0, rows, 0, LANES:k] * w_rows[0]
        for b in range(1, bands):
            total += psf[b, rows, 0, LANES:k] * w_rows[b]
        comb[3, rows, :] = total

    h = size // 2
    inputs[1].wait()
    side[0] = pack(coeffs[0, 0, 0:h, 0:LANES], coeffs[0, 0, h:size, 0:LANES], True)
    side[1] = pack(
        coeffs[0, 0, 0:h, size - LANES : size], coeffs[0, 0, h:size, size - LANES : size], False
    )
    for i, top in enumerate((0, size - B)):
        for j in range(2):
            lanes = slice(0, LANES) if j == 0 else slice(size - LANES, size)
            corner[2 * i + j] = pack(
                coeffs[0, 0, top : top + B // 2, lanes],
                coeffs[0, 0, top + B // 2 : top + B, lanes],
                j == 0,
            )

    def halo(d):
        dr, dc = d
        if dr == 0:
            i = (dc + 1) // 2
            src, dst = side.at[i], side_in.at[i]
        elif dc == 0:
            i = (dr + 1) // 2
            src = coeffs.at[0, 0, pl.ds(i * (size - B), B), :]
            dst = vert_in.at[i]
        else:
            i = (dr + 1) + (dc + 1) // 2
            src, dst = corner.at[i], corner_in.at[i]
        n = NEIGHBOURS.index(d)
        return pltpu.make_async_remote_copy(
            src, dst, halo_send.at[n], halo_recv.at[n], device_id=device(d)
        )

    pl.semaphore_wait(barrier, count)

    def to_sib(src, dst, i):
        return pltpu.make_async_remote_copy(src, dst, s_send.at[i], s_recv.at[i], device_id=sib)

    later = jnp.where(chip == 0, 6, 4)
    a_copies = [to_sib(comb.at[2 * (1 - core) + i], recv_a.at[i], i) for i in range(2)]
    a_copies.append(to_sib(comb.at[later + 1 - core], recv_a.at[2], 2))
    b_copies = [to_sib(comb.at[pl.ds(4 * i, 4)], recv_b.at[pl.ds(4 * i, 4)], 3 + i) for i in range(2)]
    a_copies[0].start()
    a_copies[1].start()
    for d in sorted(NEIGHBOURS, key=lambda d: abs(d[0]) + abs(d[1]) == 2):
        @pl.when(exists(d))
        def _():
            halo(d).start()

    a_copies[2].start()
    b_copies[0].start()
    b_copies[1].start()

    x_copies, f_copies = [], []
    for i in range(3):
        slot = xrecv.at[2 * core + i if i < 2 else 4 + core]
        x_copies.append(
            pltpu.make_async_remote_copy(fsum.at[i], slot, x_send.at[i], x_recv.at[i], device_id=far)
        )
        f_copies.append(
            pltpu.make_async_remote_copy(slot, slot, f_send.at[i], f_recv.at[i], device_id=sib)
        )
        a_copies[i].wait_recv()
        fsum[i] = comb[2 * core + i if i < 2 else later + core] + recv_a[i]
        x_copies[i].start()

    away, home = 2 * (1 - chip), 2 * chip
    terms = (away + 1 - core, away + core, home + 1 - core, home + core)

    def weight(b, t):
        w = powers[b]
        return jnp.where(t == 0, w[0], jnp.where(t == 1, w[1], jnp.where(t == 2, w[2], w[3])))

    kright[:, 3 * KROWS : 512] = jnp.zeros((2, 512 - 3 * KROWS, 2 * HC), BF16)
    zright[6 * HR : 1280] = jnp.zeros((1280 - 6 * HR, 2 * HC), BF16)
    put_left(xo, lambda rows: coeffs[0, 0, rows], size)
    local[1].wait()
    own_part[...] = dot(xo[0:size], fo[...])
    local[0].wait()
    for r in range(0, size, 32):
        rows = slice(r, r + 32)
        planes = [dirty[n, 0, rows] for n in range(bands)]
        for i, t in enumerate(terms):
            total = planes[0] * weight(0, t)
            for n in range(1, bands):
                total += planes[n] * weight(n, t)
            dsum[i, rows] = total

    for copy in local[2:]:
        copy.wait()

    for i in range(2):
        x_copies[i].wait_recv()
        f_copies[i].start()

    for d in NEIGHBOURS:
        dr, dc = d
        there = exists(d)
        incoming = halo((-dr, -dc))

        @pl.when(there)
        def _():
            incoming.wait_recv()

        if dr == 0:
            ref, i = side_in, (1 - dc) // 2
        elif dc == 0:
            ref, i = vert_in, (1 - dr) // 2
        else:
            ref, i = corner_in, (1 - dr) + (1 - dc) // 2

        @pl.when(jnp.logical_not(there))
        def _():
            ref[i] = jnp.zeros(ref.shape[1:], F32)

    def edge(right, left, m):
        top = jnp.where(m, right, left)
        bottom = pltpu.roll(jnp.where(m, left, right), LANES // 2, 1)
        return jnp.concatenate([top, bottom], axis=0)

    def place(ref, x, row, step):
        put_left(ref, lambda rows: x[rows], x.shape[0], row, step)

    place(xe, edge(side_in[0], side_in[1], half_mask((h, LANES))), 0, 64)
    small = half_mask((B // 2, LANES))
    for i in range(2):
        put_left(xo, lambda rows: vert_in[i, rows], B, size + i * B)
        place(xe, edge(corner_in[2 * i], corner_in[2 * i + 1], small), size + i * B, 64)
    total_rows = size + 2 * B
    acc[0:size] = own_part[...] + dot(xe[0:size], fe[...])
    acc[size:total_rows] = dot(xo[size:], fo[...]) + dot(xe[size:], fe[...])
    put_right(yr, lambda rows: acc[rows], total_rows, total_rows)
    acc[...] = dot(fr[...], yr[...])

    def halves(load, rows):
        below = slice(HR + rows.start, HR + rows.stop)
        cc, cs = load(rows, slice(0, HC)), load(rows, slice(HC, 2 * HC))
        sc, ss = load(below, slice(0, HC)), load(below, slice(HC, 2 * HC))
        return cc - ss, sc + cs, cc + ss, sc - cs

    for r in range(0, HR, 16):
        rows = slice(r, r + 16)
        for n, x in enumerate(halves(lambda a, b: acc[a, b], rows)):
            field[n, rows] = x

    def forwarded(i):
        other = xrecv.at[2 * (1 - core) + i if i < 2 else 5 - core]
        pltpu.make_async_remote_copy(
            other, other, f_send.at[i], f_recv.at[i], device_id=sib
        ).wait_recv()

    blank = jnp.zeros((KROWS - SENT, 2 * LANES), F32)

    def kernels(first):
        column = comb[3] + recv_b[3] + xrecv[3]
        for i in range(2):
            s = g + terms[first + i]
            at = jnp.where(s < 2, s + 4, jnp.where(s < 5, s - 2, s + 1))
            slot = jnp.where(s < 2, s + 4, jnp.where(s < 5, s - 2, s - 1))
            main = comb[at] + recv_b[at] + xrecv[slot]
            last = jnp.where(lane == s, column, 0.0)
            block = jnp.concatenate([main, last], axis=1)
            place(pleft, jnp.concatenate([block, blank], axis=0), i * KROWS, 16)
        kacc[...] = dot(pleft[...], kc[...])
        for i in range(2):
            put_right(
                kright.at[i],
                lambda rows: kacc[i * KROWS + rows.start : i * KROWS + rows.stop],
                KROWS, KROWS,
            )
            kern[i] = dot(kr[...], kright[i])

    def term(i, put):
        for r in range(0, HR, 16):
            rows = slice(r, r + 16)
            a, b, c, d = (field[n, rows] for n in range(4))
            e, f, p, q = halves(lambda u, v: kern[i % 2, u, v], rows)
            re1, im1 = a * e - b * f, a * f + b * e
            re2, im2 = c * p - d * q, c * q + d * p
            parts = ((re1 + re2, im1 - im2), (im1 + im2, re2 - re1))
            for m in range(2):
                for n in range(2):
                    hi, lo = split(parts[m][n])
                    lanes = slice(n * HC, (n + 1) * HC)
                    at = m * HR + r
                    zright[at : at + 16, lanes] = hi
                    zright[2 * HR + at : 2 * HR + at + 16, lanes] = lo
                    zright[4 * HR + at : 4 * HR + at + 16, lanes] = hi
        acc[0:size] = dot(br[...], zright[...])
        put_left(wleft, lambda rows: acc[rows], size)
        for j in range(2):
            rows = slice(j * h, (j + 1) * h)
            put(j, rows, dsum[i, rows] - dot(wleft[rows], bc[...]))

    def pair_copy(i, j):
        n = 2 * i + j
        rows = pl.ds(j * h, h)
        return pltpu.make_async_remote_copy(
            part.at[i, rows], pair_in.at[i, rows], t_send.at[n], t_recv.at[n], device_id=sib
        )

    def cross_copy(j):
        rows = pl.ds(j * h, h)
        return pltpu.make_async_remote_copy(
            term_x.at[rows], term_in.at[rows], t_send.at[4 + j], t_recv.at[4 + j], device_id=far
        )

    pairs = [[pair_copy(i, j) for j in range(2)] for i in range(2)]
    crosses = [cross_copy(j) for j in range(2)]

    def to_pair(i):
        def put(j, rows, value):
            part[i, rows] = value
            pairs[i][j].start()

        return put

    def to_far(j, rows, value):
        pairs[0][j].wait_recv()
        term_x[rows] = value + pair_in[0, rows]
        crosses[j].start()

    def to_out(j, rows, value):
        pairs[1][j].wait_recv()
        out[0, 0, rows] = value + pair_in[1, rows]

    forwarded(0)
    forwarded(1)
    b_copies[0].wait_recv()
    kernels(0)
    x_copies[2].wait_recv()
    f_copies[2].start()
    term(0, to_pair(0))
    term(1, to_far)
    forwarded(2)
    b_copies[1].wait_recv()
    kernels(2)
    term(2, to_pair(1))
    term(3, to_out)
    for j in range(2):
        rows = slice(j * h, (j + 1) * h)
        crosses[j].wait_recv()
        got[0, 0, rows] = term_in[rows]

    for d in NEIGHBOURS:
        @pl.when(exists(d))
        def _():
            halo(d).wait_send()

    for copy in (*a_copies, *b_copies, *x_copies, *f_copies, *pairs[0], *pairs[1], *crosses):
        copy.wait_send()


def body(coeffs, dirty, psf, band_offset):
    size = coeffs.shape[-1]
    span = size + 2 * B
    bands = dirty.shape[0]
    psf = psf.transpose(0, 2, 1, 3)
    facets = lax.axis_size("facet")
    consts = tables(size, span, psf.shape[-1])
    vmem = pl.BlockSpec(memory_space=pltpu.VMEM)
    hbm = pl.BlockSpec(memory_space=pltpu.HBM)
    dma = lambda n: pltpu.SemaphoreType.DMA((n,))
    scratch = [pltpu.VMEM(c.shape, BF16) for c in consts]
    scratch += [
        pltpu.VMEM(coeffs.shape, F32),
        pltpu.VMEM(dirty.shape, F32),
        pltpu.VMEM(psf.shape, F32),
        pltpu.VMEM((2 * HR, 2 * HC), F32),
        pltpu.VMEM((2 * KROWS, 2 * HC), F32),
        dma(10),
        pltpu.VMEM((8, SENT, LANES), F32),
        pltpu.VMEM((3, SENT, LANES), F32),
        pltpu.VMEM((8, SENT, LANES), F32),
        pltpu.VMEM((3, SENT, LANES), F32),
        pltpu.VMEM((6, SENT, LANES), F32),
        pltpu.VMEM((2, size // 2, LANES), F32),
        pltpu.VMEM((2, size // 2, LANES), F32),
        pltpu.VMEM((4, B // 2, LANES), F32),
        pltpu.VMEM((4, B // 2, LANES), F32),
        pltpu.VMEM((2, B, size), F32),
        pltpu.VMEM((span, 3 * size), BF16),
        pltpu.VMEM((span, 3 * LANES), BF16),
        pltpu.VMEM((size, 2 * HC), F32),
        pltpu.VMEM((3 * span, 2 * HC), BF16),
        pltpu.VMEM((2 * KROWS, 6 * LANES), BF16),
        pltpu.VMEM((2, 512, 2 * HC), BF16),
        pltpu.VMEM((1280, 2 * HC), BF16),
        pltpu.VMEM((size, 6 * HC), BF16),
        pltpu.VMEM((4, HR, HC), F32),
        pltpu.VMEM((2, 2 * HR, 2 * HC), F32),
        pltpu.VMEM((TERMS, size, size), F32),
        pltpu.VMEM((2, size, size), F32),
        pltpu.VMEM((2, size, size), F32),
        pltpu.VMEM((size, size), F32),
        pltpu.VMEM((size, size), F32),
        dma(8), dma(8), dma(5), dma(5), dma(3), dma(3), dma(3), dma(3), dma(6), dma(6),
    ]

    def run(*args):
        kernel(facets, size, bands, *args)

    shape = jax.ShapeDtypeStruct(coeffs.shape, F32)
    kept, received = pl.pallas_call(
        run,
        out_shape=(shape, shape),
        in_specs=[hbm, hbm, hbm, pl.BlockSpec(memory_space=pltpu.SMEM)] + [hbm] * 7,
        out_specs=(vmem, vmem),
        scratch_shapes=scratch,
        compiler_params=pltpu.CompilerParams(
            collective_id=0, has_side_effects=True, vmem_limit_bytes=24 * 1024 * 1024
        ),
        cost_estimate=pl.CostEstimate(flops=4_000_000_000, bytes_accessed=8_000_000, transcendentals=0),
    )(coeffs, dirty, psf, band_offset, *[jnp.asarray(c) for c in consts])
    return kept + received


def solution(mesh):
    placed = (
        P("band", "facet", None, None),
        P("band", "facet", None, None),
        P("band", "facet", None, None),
        P("band"),
    )
    return jax.shard_map(
        body, mesh=mesh, in_specs=placed, out_specs=P("band", "facet", None, None), check_vma=False
    )
```

```python
import ml_dtypes
import numpy as np
import jax
import jax.numpy as jnp
from jax import lax
from jax.experimental import pallas as pl
from jax.experimental.pallas import tpu as pltpu
from jax.sharding import PartitionSpec as P

B = 64
TERMS = 4
FGY = 4
POWERS = 2 * TERMS - 1
ORDER = (2, 3, 4, None, 0, 1, 5, 6)
HR = 208
HC = 256
KROWS = 144
SENT = 136
LANES = 128
F32 = jnp.float32
BF16 = jnp.bfloat16
NEIGHBOURS = [(dr, dc) for dr in (-1, 0, 1) for dc in (-1, 0, 1) if (dr, dc) != (0, 0)]


def forward_table(positions, length, half):
    k = np.arange(half)
    angle = 2 * np.pi * ((k[:, None] * positions[None, :]) % length) / length
    ok = (k <= length // 2)[:, None]
    return np.concatenate([np.cos(angle) * ok, np.sin(angle) * ok], axis=0)


def inverse_table(positions, length, half):
    k = np.arange(half)
    fold = np.where((k == 0) | (k == length // 2), 1.0, 2.0) / length
    return forward_table(positions, length, half) * np.concatenate([fold, fold])[:, None]


def split_table(table):
    hi = table.astype(np.float32).astype(ml_dtypes.bfloat16)
    lo = (table - hi.astype(np.float64)).astype(np.float32).astype(ml_dtypes.bfloat16)
    return hi, lo


def left_table(table, width):
    hi, lo = split_table(table)
    whole = np.concatenate([hi, hi, lo], axis=1)
    return np.pad(whole, ((0, 0), (0, width - whole.shape[1])))


def right_table(table):
    hi, lo = split_table(table)
    return np.concatenate([hi, lo, hi], axis=0)


def tables(size, span, k):
    pos = np.arange(span)
    out = np.arange(size)
    ker = np.arange(k) - B
    cols = forward_table(pos, span, HC).T
    field_own, field_edge = right_table(cols[:size]), right_table(cols[size:])
    field_rows = left_table(forward_table(pos, span, HR), 3 * span)
    kern = forward_table(ker, span, HC).T
    kern = np.concatenate([kern[:LANES], np.repeat(kern[LANES:], LANES, axis=0)], axis=0)
    kern_cols = right_table(kern)
    rows = np.pad(forward_table(ker, span, HR), ((0, 0), (0, KROWS - k)))
    kern_rows = left_table(rows, 512)
    back_rows = left_table(inverse_table(out, span, HR).T / 2, 1280)
    back_cols = right_table(inverse_table(out, span, HC))
    return field_own, field_edge, field_rows, kern_cols, kern_rows, back_rows, back_cols


def split(x):
    hi = x.astype(BF16)
    return hi, (x - hi.astype(F32)).astype(BF16)


def put_left(ref, load, height, row=0, step=16):
    for r in range(0, height, step):
        x = load(slice(r, r + step))
        hi, lo = split(x)
        w = x.shape[1]
        rows = slice(row + r, row + r + step)
        ref[rows, 0:w] = hi
        ref[rows, w : 2 * w] = hi
        ref[rows, 2 * w : 3 * w] = lo


def put_right(ref, load, height, pitch, step=16):
    for r in range(0, height, step):
        hi, lo = split(load(slice(r, r + step)))
        ref[r : r + step] = hi
        ref[pitch + r : pitch + r + step] = lo
        ref[2 * pitch + r : 2 * pitch + r + step] = hi


def dot(a, b):
    return jnp.dot(a, b, preferred_element_type=F32)


def half_mask(shape):
    return lax.broadcasted_iota(jnp.int32, shape, 1) < LANES // 2


def pack(first, second, left):
    mask = half_mask(first.shape)
    moved = pltpu.roll(second, LANES // 2, 1)
    return jnp.where(mask, first, moved) if left else jnp.where(mask, moved, first)


def kernel(
    facets, size, bands,
    coeffs_hbm, dirty_hbm, psf_hbm, offset, *refs,
):
    tables_hbm = refs[:7]
    out, got = refs[7:9]
    (fo, fe, fr, kc, kr, br, bc, coeffs, dirty, psf, acc, kacc, local_sem,
     comb, recv_a, recv_b, fsum, xrecv, side, side_in, corner, corner_in, vert_in,
     xo, xe, own_part, yr, pleft, kright, zright, wleft, field, kern, dsum, part, pair_in, term_x,
     term_in, halo_send, halo_recv, s_send, s_recv, x_send, x_recv, f_send, f_recv,
     t_send, t_recv) = refs[9:]
    vm = (fo, fe, fr, kc, kr, br, bc)

    g = lax.axis_index("band")
    facet = lax.axis_index("facet")
    chip, core = g // 2, g % 2
    sib = {"band": 2 * chip + 1 - core}
    far = {"band": 2 * (1 - chip) + core}
    q = (facet + FGY + FGY // 2) % facets
    row, col = q // FGY, q % FGY

    def exists(d):
        r, c = row + d[0], col + d[1]
        return (r >= 0) & (r < facets // FGY) & (c >= 0) & (c < FGY)

    def device(d):
        return {"facet": (facet + FGY * d[0] + d[1] + facets) % facets}

    inputs = [
        pltpu.make_async_copy(psf_hbm, psf, local_sem.at[8]),
        pltpu.make_async_copy(coeffs_hbm, coeffs, local_sem.at[9]),
    ]
    for copy in inputs:
        copy.start()

    barrier = pltpu.get_barrier_semaphore()
    count = 2
    for d in NEIGHBOURS:
        there = exists(d)
        count = count + there.astype(jnp.int32)

        @pl.when(there)
        def _():
            pl.semaphore_signal(barrier, inc=1, device_id=device(d))

    for peer in (sib, far):
        pl.semaphore_signal(barrier, inc=1, device_id=peer)

    local = [pltpu.make_async_copy(dirty_hbm, dirty, local_sem.at[7])]
    local += [pltpu.make_async_copy(tables_hbm[i], vm[i], local_sem.at[i]) for i in range(7)]
    for copy in local:
        copy.start()

    powers = []
    for b in range(bands):
        w = offset[b]
        row_b = [jnp.float32(1.0)]
        for _ in range(1, POWERS):
            row_b.append(row_b[-1] * w)
        powers.append(row_b)

    k = psf.shape[1]
    lane = lax.broadcasted_iota(jnp.int32, (1, LANES), 1)
    comb[:, LANES:SENT, :] = jnp.zeros((8, SENT - LANES, LANES), F32)
    w_rows = []
    for b in range(bands):
        w_row = jnp.zeros((1, LANES), F32)
        for s in range(POWERS):
            w_row = jnp.where(lane == s, powers[b][s], w_row)
        w_rows.append(w_row)
    def combine(wanted, with_last):
        for top in range(0, k, 32):
            rows = slice(top, min(top + 32, k))
            planes = [psf[b, rows, 0, 0:LANES] for b in range(bands)]
            for s in wanted:
                total = planes[0]
                if s:
                    total = total * powers[0][s]
                for b in range(1, bands):
                    total += planes[b] * powers[b][s]
                comb[ORDER.index(s), rows, :] = total
            if with_last:
                total = psf[0, rows, 0, LANES:k] * w_rows[0]
                for b in range(1, bands):
                    total += psf[b, rows, 0, LANES:k] * w_rows[b]
                comb[3, rows, :] = total

    h = size // 2
    inputs[1].wait()
    side[0] = pack(coeffs[0, 0, 0:h, 0:LANES], coeffs[0, 0, h:size, 0:LANES], True)
    side[1] = pack(
        coeffs[0, 0, 0:h, size - LANES : size], coeffs[0, 0, h:size, size - LANES : size], False
    )
    for i, top in enumerate((0, size - B)):
        for j in range(2):
            lanes = slice(0, LANES) if j == 0 else slice(size - LANES, size)
            corner[2 * i + j] = pack(
                coeffs[0, 0, top : top + B // 2, lanes],
                coeffs[0, 0, top + B // 2 : top + B, lanes],
                j == 0,
            )

    def halo(d):
        dr, dc = d
        if dr == 0:
            i = (dc + 1) // 2
            src, dst = side.at[i], side_in.at[i]
        elif dc == 0:
            i = (dr + 1) // 2
            src = coeffs.at[0, 0, pl.ds(i * (size - B), B), :]
            dst = vert_in.at[i]
        else:
            i = (dr + 1) + (dc + 1) // 2
            src, dst = corner.at[i], corner_in.at[i]
        n = NEIGHBOURS.index(d)
        return pltpu.make_async_remote_copy(
            src, dst, halo_send.at[n], halo_recv.at[n], device_id=device(d)
        )

    inputs[0].wait()
    combine((2, 3, 4), True)
    pl.semaphore_wait(barrier, count)

    def to_sib(src, dst, i):
        return pltpu.make_async_remote_copy(src, dst, s_send.at[i], s_recv.at[i], device_id=sib)

    later = jnp.where(chip == 0, 6, 4)
    a_copies = [to_sib(comb.at[2 * (1 - core) + i], recv_a.at[i], i) for i in range(2)]
    a_copies.append(to_sib(comb.at[later + 1 - core], recv_a.at[2], 2))
    b_copies = [to_sib(comb.at[pl.ds(4 * i, 4)], recv_b.at[pl.ds(4 * i, 4)], 3 + i) for i in range(2)]
    a_copies[0].start()
    a_copies[1].start()
    for d in sorted(NEIGHBOURS, key=lambda d: abs(d[0]) + abs(d[1]) == 2):
        @pl.when(exists(d))
        def _():
            halo(d).start()

    x_copies, f_copies = [], []

    def cross_kernel(i):
        slot = xrecv.at[2 * core + i if i < 2 else 4 + core]
        x_copies.append(
            pltpu.make_async_remote_copy(fsum.at[i], slot, x_send.at[i], x_recv.at[i], device_id=far)
        )
        f_copies.append(
            pltpu.make_async_remote_copy(slot, slot, f_send.at[i], f_recv.at[i], device_id=sib)
        )
        a_copies[i].wait_recv()
        fsum[i] = comb[2 * core + i if i < 2 else later + core] + recv_a[i]
        x_copies[i].start()

    cross_kernel(0)
    cross_kernel(1)
    combine((0, 1, 5, 6), False)
    a_copies[2].start()
    b_copies[0].start()
    b_copies[1].start()
    cross_kernel(2)

    away, home = 2 * (1 - chip), 2 * chip
    terms = (away + 1 - core, away + core, home + 1 - core, home + core)

    def weight(b, t):
        w = powers[b]
        return jnp.where(t == 0, w[0], jnp.where(t == 1, w[1], jnp.where(t == 2, w[2], w[3])))

    kright[:, 3 * KROWS : 512] = jnp.zeros((2, 512 - 3 * KROWS, 2 * HC), BF16)
    zright[6 * HR : 1280] = jnp.zeros((1280 - 6 * HR, 2 * HC), BF16)
    put_left(xo, lambda rows: coeffs[0, 0, rows], size)
    local[1].wait()
    own_part[...] = dot(xo[0:size], fo[...])
    local[0].wait()
    for r in range(0, size, 32):
        rows = slice(r, r + 32)
        planes = [dirty[n, 0, rows] for n in range(bands)]
        for i, t in enumerate(terms):
            total = planes[0] * weight(0, t)
            for n in range(1, bands):
                total += planes[n] * weight(n, t)
            dsum[i, rows] = total

    for copy in local[2:]:
        copy.wait()

    for i in range(2):
        x_copies[i].wait_recv()
        f_copies[i].start()

    for d in NEIGHBOURS:
        dr, dc = d
        there = exists(d)
        incoming = halo((-dr, -dc))

        @pl.when(there)
        def _():
            incoming.wait_recv()

        if dr == 0:
            ref, i = side_in, (1 - dc) // 2
        elif dc == 0:
            ref, i = vert_in, (1 - dr) // 2
        else:
            ref, i = corner_in, (1 - dr) + (1 - dc) // 2

        @pl.when(jnp.logical_not(there))
        def _():
            ref[i] = jnp.zeros(ref.shape[1:], F32)

    def edge(right, left, m):
        top = jnp.where(m, right, left)
        bottom = pltpu.roll(jnp.where(m, left, right), LANES // 2, 1)
        return jnp.concatenate([top, bottom], axis=0)

    def place(ref, x, row, step):
        put_left(ref, lambda rows: x[rows], x.shape[0], row, step)

    place(xe, edge(side_in[0], side_in[1], half_mask((h, LANES))), 0, 64)
    small = half_mask((B // 2, LANES))
    for i in range(2):
        put_left(xo, lambda rows: vert_in[i, rows], B, size + i * B)
        place(xe, edge(corner_in[2 * i], corner_in[2 * i + 1], small), size + i * B, 64)
    total_rows = size + 2 * B
    acc[0:size] = own_part[...] + dot(xe[0:size], fe[...])
    acc[size:total_rows] = dot(xo[size:], fo[...]) + dot(xe[size:], fe[...])
    put_right(yr, lambda rows: acc[rows], total_rows, total_rows)
    acc[...] = dot(fr[...], yr[...])

    def halves(load, rows):
        below = slice(HR + rows.start, HR + rows.stop)
        cc, cs = load(rows, slice(0, HC)), load(rows, slice(HC, 2 * HC))
        sc, ss = load(below, slice(0, HC)), load(below, slice(HC, 2 * HC))
        return cc - ss, sc + cs, cc + ss, sc - cs

    for r in range(0, HR, 16):
        rows = slice(r, r + 16)
        for n, x in enumerate(halves(lambda a, b: acc[a, b], rows)):
            field[n, rows] = x

    def forwarded(i):
        other = xrecv.at[2 * (1 - core) + i if i < 2 else 5 - core]
        pltpu.make_async_remote_copy(
            other, other, f_send.at[i], f_recv.at[i], device_id=sib
        ).wait_recv()

    blank = jnp.zeros((KROWS - SENT, 2 * LANES), F32)

    def kernels(first):
        column = comb[3] + recv_b[3] + xrecv[3]
        for i in range(2):
            s = g + terms[first + i]
            at = jnp.where(s < 2, s + 4, jnp.where(s < 5, s - 2, s + 1))
            slot = jnp.where(s < 2, s + 4, jnp.where(s < 5, s - 2, s - 1))
            main = comb[at] + recv_b[at] + xrecv[slot]
            last = jnp.where(lane == s, column, 0.0)
            block = jnp.concatenate([main, last], axis=1)
            place(pleft, jnp.concatenate([block, blank], axis=0), i * KROWS, 16)
        kacc[...] = dot(pleft[...], kc[...])
        for i in range(2):
            put_right(
                kright.at[i],
                lambda rows: kacc[i * KROWS + rows.start : i * KROWS + rows.stop],
                KROWS, KROWS,
            )
            kern[i] = dot(kr[...], kright[i])

    def term(i, put):
        for r in range(0, HR, 16):
            rows = slice(r, r + 16)
            a, b, c, d = (field[n, rows] for n in range(4))
            e, f, p, q = halves(lambda u, v: kern[i % 2, u, v], rows)
            re1, im1 = a * e - b * f, a * f + b * e
            re2, im2 = c * p - d * q, c * q + d * p
            parts = ((re1 + re2, im1 - im2), (im1 + im2, re2 - re1))
            for m in range(2):
                for n in range(2):
                    hi, lo = split(parts[m][n])
                    lanes = slice(n * HC, (n + 1) * HC)
                    at = m * HR + r
                    zright[at : at + 16, lanes] = hi
                    zright[2 * HR + at : 2 * HR + at + 16, lanes] = lo
                    zright[4 * HR + at : 4 * HR + at + 16, lanes] = hi
        acc[0:size] = dot(br[...], zright[...])
        put_left(wleft, lambda rows: acc[rows], size)
        for j in range(2):
            rows = slice(j * h, (j + 1) * h)
            put(j, rows, dsum[i, rows] - dot(wleft[rows], bc[...]))

    def pair_copy(i, j):
        n = 2 * i + j
        rows = pl.ds(j * h, h)
        return pltpu.make_async_remote_copy(
            part.at[i, rows], pair_in.at[i, rows], t_send.at[n], t_recv.at[n], device_id=sib
        )

    def cross_copy(j):
        rows = pl.ds(j * h, h)
        return pltpu.make_async_remote_copy(
            term_x.at[rows], term_in.at[rows], t_send.at[4 + j], t_recv.at[4 + j], device_id=far
        )

    pairs = [[pair_copy(i, j) for j in range(2)] for i in range(2)]
    crosses = [cross_copy(j) for j in range(2)]

    def to_pair(i):
        def put(j, rows, value):
            part[i, rows] = value
            pairs[i][j].start()

        return put

    def to_far(j, rows, value):
        pairs[0][j].wait_recv()
        term_x[rows] = value + pair_in[0, rows]
        crosses[j].start()

    def to_out(j, rows, value):
        pairs[1][j].wait_recv()
        out[0, 0, rows] = value + pair_in[1, rows]

    forwarded(0)
    forwarded(1)
    b_copies[0].wait_recv()
    kernels(0)
    x_copies[2].wait_recv()
    f_copies[2].start()
    term(0, to_pair(0))
    term(1, to_far)
    forwarded(2)
    b_copies[1].wait_recv()
    kernels(2)
    term(2, to_pair(1))
    term(3, to_out)
    for j in range(2):
        rows = slice(j * h, (j + 1) * h)
        crosses[j].wait_recv()
        got[0, 0, rows] = term_in[rows]

    for d in NEIGHBOURS:
        @pl.when(exists(d))
        def _():
            halo(d).wait_send()

    for copy in (*a_copies, *b_copies, *x_copies, *f_copies, *pairs[0], *pairs[1], *crosses):
        copy.wait_send()


def body(coeffs, dirty, psf, band_offset):
    size = coeffs.shape[-1]
    span = size + 2 * B
    bands = dirty.shape[0]
    psf = psf.transpose(0, 2, 1, 3)
    facets = lax.axis_size("facet")
    consts = tables(size, span, psf.shape[-1])
    vmem = pl.BlockSpec(memory_space=pltpu.VMEM)
    hbm = pl.BlockSpec(memory_space=pltpu.HBM)
    dma = lambda n: pltpu.SemaphoreType.DMA((n,))
    scratch = [pltpu.VMEM(c.shape, BF16) for c in consts]
    scratch += [
        pltpu.VMEM(coeffs.shape, F32),
        pltpu.VMEM(dirty.shape, F32),
        pltpu.VMEM(psf.shape, F32),
        pltpu.VMEM((2 * HR, 2 * HC), F32),
        pltpu.VMEM((2 * KROWS, 2 * HC), F32),
        dma(10),
        pltpu.VMEM((8, SENT, LANES), F32),
        pltpu.VMEM((3, SENT, LANES), F32),
        pltpu.VMEM((8, SENT, LANES), F32),
        pltpu.VMEM((3, SENT, LANES), F32),
        pltpu.VMEM((6, SENT, LANES), F32),
        pltpu.VMEM((2, size // 2, LANES), F32),
        pltpu.VMEM((2, size // 2, LANES), F32),
        pltpu.VMEM((4, B // 2, LANES), F32),
        pltpu.VMEM((4, B // 2, LANES), F32),
        pltpu.VMEM((2, B, size), F32),
        pltpu.VMEM((span, 3 * size), BF16),
        pltpu.VMEM((span, 3 * LANES), BF16),
        pltpu.VMEM((size, 2 * HC), F32),
        pltpu.VMEM((3 * span, 2 * HC), BF16),
        pltpu.VMEM((2 * KROWS, 6 * LANES), BF16),
        pltpu.VMEM((2, 512, 2 * HC), BF16),
        pltpu.VMEM((1280, 2 * HC), BF16),
        pltpu.VMEM((size, 6 * HC), BF16),
        pltpu.VMEM((4, HR, HC), F32),
        pltpu.VMEM((2, 2 * HR, 2 * HC), F32),
        pltpu.VMEM((TERMS, size, size), F32),
        pltpu.VMEM((2, size, size), F32),
        pltpu.VMEM((2, size, size), F32),
        pltpu.VMEM((size, size), F32),
        pltpu.VMEM((size, size), F32),
        dma(8), dma(8), dma(5), dma(5), dma(3), dma(3), dma(3), dma(3), dma(6), dma(6),
    ]

    def run(*args):
        kernel(facets, size, bands, *args)

    shape = jax.ShapeDtypeStruct(coeffs.shape, F32)
    kept, received = pl.pallas_call(
        run,
        out_shape=(shape, shape),
        in_specs=[hbm, hbm, hbm, pl.BlockSpec(memory_space=pltpu.SMEM)] + [hbm] * 7,
        out_specs=(vmem, vmem),
        scratch_shapes=scratch,
        compiler_params=pltpu.CompilerParams(
            collective_id=0, has_side_effects=True, vmem_limit_bytes=54592 * 1024
        ),
        cost_estimate=pl.CostEstimate(flops=4_000_000_000, bytes_accessed=8_000_000, transcendentals=0),
    )(coeffs, dirty, psf, band_offset, *[jnp.asarray(c) for c in consts])
    return kept + received


def solution(mesh):
    placed = (
        P("band", "facet", None, None),
        P("band", "facet", None, None),
        P("band", "facet", None, None),
        P("band"),
    )
    return jax.shard_map(
        body, mesh=mesh, in_specs=placed, out_specs=P("band", "facet", None, None), check_vma=False
    )
```

```python
import ml_dtypes
import numpy as np
import jax
import jax.numpy as jnp
from jax import lax
from jax.experimental import pallas as pl
from jax.experimental.pallas import tpu as pltpu
from jax.sharding import PartitionSpec as P

B = 64
TERMS = 4
FGY = 4
POWERS = 2 * TERMS - 1
EARLY = (2, 3, 4)
LATE = (0, 1, 5, 6)
HR = 208
HC = 256
KROWS = 144
SENT = 136
TURNED = 3 * SENT
SHARE = 216
PIECES = ((0, 112), (112, 104))
LANES = 128
F32 = jnp.float32
BF16 = jnp.bfloat16
NEIGHBOURS = [(dr, dc) for dr in (-1, 0, 1) for dc in (-1, 0, 1) if (dr, dc) != (0, 0)]


def forward_table(positions, length, half):
    k = np.arange(half)
    angle = 2 * np.pi * ((k[:, None] * positions[None, :]) % length) / length
    ok = (k <= length // 2)[:, None]
    return np.concatenate([np.cos(angle) * ok, np.sin(angle) * ok], axis=0)


def inverse_table(positions, length, half):
    k = np.arange(half)
    fold = np.where((k == 0) | (k == length // 2), 1.0, 2.0) / length
    return forward_table(positions, length, half) * np.concatenate([fold, fold])[:, None]


def split_table(table):
    hi = table.astype(np.float32).astype(ml_dtypes.bfloat16)
    lo = (table - hi.astype(np.float64)).astype(np.float32).astype(ml_dtypes.bfloat16)
    return hi, lo


def left_table(table, width):
    hi, lo = split_table(table)
    whole = np.concatenate([hi, hi, lo], axis=1)
    return np.pad(whole, ((0, 0), (0, width - whole.shape[1])))


def right_table(table):
    hi, lo = split_table(table)
    return np.concatenate([hi, lo, hi], axis=0)


def tables(size, span, k):
    pos = np.arange(span)
    out = np.arange(size)
    ker = np.arange(k) - B
    cols = forward_table(pos, span, HC).T
    field_own, field_edge = right_table(cols[:size]), right_table(cols[size:])
    field_rows = left_table(forward_table(pos, span, HR), 3 * span)
    kern = forward_table(ker, span, HC).T
    kern = np.concatenate([kern[:LANES], np.repeat(kern[LANES:], LANES, axis=0)], axis=0)
    kern_cols = right_table(kern)
    rows = np.pad(forward_table(ker, span, HR), ((0, 0), (0, KROWS - k)))
    kern_rows = left_table(rows, 512)
    back_rows = left_table(inverse_table(out, span, HR).T / 2, 1280)
    back_cols = right_table(inverse_table(out, span, HC))
    return field_own, field_edge, field_rows, kern_cols, kern_rows, back_rows, back_cols


def split(x):
    hi = x.astype(BF16)
    return hi, (x - hi.astype(F32)).astype(BF16)


def put_left(ref, load, height, row=0, step=16):
    for r in range(0, height, step):
        x = load(slice(r, r + step))
        hi, lo = split(x)
        w = x.shape[1]
        rows = slice(row + r, row + r + step)
        ref[rows, 0:w] = hi
        ref[rows, w : 2 * w] = hi
        ref[rows, 2 * w : 3 * w] = lo


def put_right(ref, load, height, pitch, step=16):
    for r in range(0, height, step):
        hi, lo = split(load(slice(r, r + step)))
        ref[r : r + step] = hi
        ref[pitch + r : pitch + r + step] = lo
        ref[2 * pitch + r : 2 * pitch + r + step] = hi


def dot(a, b):
    return jnp.dot(a, b, preferred_element_type=F32)


def half_mask(shape):
    return lax.broadcasted_iota(jnp.int32, shape, 1) < LANES // 2


def pack(first, second, left):
    mask = half_mask(first.shape)
    moved = pltpu.roll(second, LANES // 2, 1)
    return jnp.where(mask, first, moved) if left else jnp.where(mask, moved, first)


def kernel(
    facets, size, bands,
    coeffs_hbm, dirty_hbm, psf_hbm, offset, *refs,
):
    tables_hbm = refs[:7]
    out, got = refs[7:9]
    (fo, fe, fr, kc, kr, br, bc, coeffs, dirty, psf, acc, kacc, local_sem,
     early, early_a, early_b, early_sum, early_x, late, late_a, late_b, late_sum, late_x, last,
     side, side_in, corner, corner_in, vert_in,
     xo, xe, own_part, yr, pleft, kright, zright, wleft, field, kern, dsum, part, pair_in, term_x,
     term_in, halo_send, halo_recv, s_send, s_recv, x_send, x_recv, f_send, f_recv,
     t_send, t_recv) = refs[9:]
    vm = (fo, fe, fr, kc, kr, br, bc)

    g = lax.axis_index("band")
    facet = lax.axis_index("facet")
    chip, core = g // 2, g % 2
    sib = {"band": 2 * chip + 1 - core}
    far = {"band": 2 * (1 - chip) + core}
    q = (facet + FGY + FGY // 2) % facets
    row, col = q // FGY, q % FGY

    def exists(d):
        r, c = row + d[0], col + d[1]
        return (r >= 0) & (r < facets // FGY) & (c >= 0) & (c < FGY)

    def device(d):
        return {"facet": (facet + FGY * d[0] + d[1] + facets) % facets}

    inputs = [
        pltpu.make_async_copy(psf_hbm, psf, local_sem.at[8]),
        pltpu.make_async_copy(coeffs_hbm, coeffs, local_sem.at[9]),
    ]
    for copy in inputs:
        copy.start()

    barrier = pltpu.get_barrier_semaphore()
    count = 2
    for d in NEIGHBOURS:
        there = exists(d)
        count = count + there.astype(jnp.int32)

        @pl.when(there)
        def _():
            pl.semaphore_signal(barrier, inc=1, device_id=device(d))

    for peer in (sib, far):
        pl.semaphore_signal(barrier, inc=1, device_id=peer)

    local = [pltpu.make_async_copy(dirty_hbm, dirty, local_sem.at[7])]
    local += [pltpu.make_async_copy(tables_hbm[i], vm[i], local_sem.at[i]) for i in range(7)]
    for copy in local:
        copy.start()

    powers = []
    for b in range(bands):
        w = offset[b]
        row_b = [jnp.float32(1.0)]
        for _ in range(1, POWERS):
            row_b.append(row_b[-1] * w)
        powers.append(row_b)

    k = psf.shape[1]
    lane = lax.broadcasted_iota(jnp.int32, (1, LANES), 1)
    tail = jnp.zeros((SENT - LANES, LANES), F32)
    for i in range(3):
        early[i * SENT + LANES : (i + 1) * SENT] = tail
    early[TURNED + 16 :] = jnp.zeros((2 * SHARE - TURNED - 16, LANES), F32)
    for i in range(4):
        late[i, LANES:SENT] = tail
    last[LANES:SENT] = tail
    w_rows = []
    for b in range(bands):
        w_row = jnp.zeros((1, LANES), F32)
        for s in range(POWERS):
            w_row = jnp.where(lane == s, powers[b][s], w_row)
        w_rows.append(w_row)
    def combine(wanted, with_last):
        for top in range(0, k, 32):
            rows = slice(top, min(top + 32, k))
            planes = [psf[b, rows, 0, 0:LANES] for b in range(bands)]
            for s in wanted:
                total = planes[0]
                if s:
                    total = total * powers[0][s]
                for b in range(1, bands):
                    total += planes[b] * powers[b][s]
                if s in EARLY:
                    at = EARLY.index(s) * SENT
                    early[at + rows.start : at + rows.stop] = total
                else:
                    late[LATE.index(s), rows] = total
            if with_last:
                total = psf[0, rows, 0, LANES:k] * w_rows[0]
                for b in range(1, bands):
                    total += psf[b, rows, 0, LANES:k] * w_rows[b]
                last[rows] = total

    h = size // 2
    inputs[1].wait()
    side[0] = pack(coeffs[0, 0, 0:h, 0:LANES], coeffs[0, 0, h:size, 0:LANES], True)
    side[1] = pack(
        coeffs[0, 0, 0:h, size - LANES : size], coeffs[0, 0, h:size, size - LANES : size], False
    )
    for i, top in enumerate((0, size - B)):
        for j in range(2):
            lanes = slice(0, LANES) if j == 0 else slice(size - LANES, size)
            corner[2 * i + j] = pack(
                coeffs[0, 0, top : top + B // 2, lanes],
                coeffs[0, 0, top + B // 2 : top + B, lanes],
                j == 0,
            )

    def halo(d):
        dr, dc = d
        if dr == 0:
            i = (dc + 1) // 2
            src, dst = side.at[i], side_in.at[i]
        elif dc == 0:
            i = (dr + 1) // 2
            src = coeffs.at[0, 0, pl.ds(i * (size - B), B), :]
            dst = vert_in.at[i]
        else:
            i = (dr + 1) + (dc + 1) // 2
            src, dst = corner.at[i], corner_in.at[i]
        n = NEIGHBOURS.index(d)
        return pltpu.make_async_remote_copy(
            src, dst, halo_send.at[n], halo_recv.at[n], device_id=device(d)
        )

    inputs[0].wait()
    combine(EARLY, True)
    early[TURNED : TURNED + 8] = jnp.transpose(last[0:LANES])[0:8]
    early[TURNED + 8 : TURNED + 16] = last[LANES:SENT]
    pl.semaphore_wait(barrier, count)

    def to_sib(src, dst, i):
        return pltpu.make_async_remote_copy(src, dst, s_send.at[i], s_recv.at[i], device_id=sib)

    away_late = jnp.where(chip == 0, 2, 0)

    def piece(i, who):
        at, rows = PIECES[i]
        return pl.ds(pl.multiple_of(SHARE * who + at, 8), rows)

    a_copies = [to_sib(early.at[piece(i, 1 - core)], early_a.at[piece(i, 0)], i) for i in range(2)]
    a_copies.append(to_sib(late.at[away_late + 1 - core], late_a, 2))
    b_copies = [to_sib(early, early_b, 3), to_sib(late, late_b, 4)]
    a_copies[0].start()
    a_copies[1].start()
    for d in sorted(NEIGHBOURS, key=lambda d: abs(d[0]) + abs(d[1]) == 2):
        @pl.when(exists(d))
        def _():
            halo(d).start()

    x_copies, f_copies = [], []
    for i in range(3):
        src, slot = late_sum, late_x.at[core]
        if i < 2:
            src, slot = early_sum.at[piece(i, 0)], early_x.at[piece(i, core)]
        x_copies.append(
            pltpu.make_async_remote_copy(src, slot, x_send.at[i], x_recv.at[i], device_id=far)
        )
        f_copies.append(
            pltpu.make_async_remote_copy(slot, slot, f_send.at[i], f_recv.at[i], device_id=sib)
        )
    for i in range(2):
        a_copies[i].wait_recv()
        early_sum[piece(i, 0)] = early[piece(i, core)] + early_a[piece(i, 0)]
        x_copies[i].start()
    combine(LATE, False)
    a_copies[2].start()
    b_copies[0].start()
    b_copies[1].start()

    away, home = 2 * (1 - chip), 2 * chip
    terms = (away + 1 - core, away + core, home + 1 - core, home + core)

    def weight(b, t):
        w = powers[b]
        return jnp.where(t == 0, w[0], jnp.where(t == 1, w[1], jnp.where(t == 2, w[2], w[3])))

    kright[:, 3 * KROWS : 512] = jnp.zeros((2, 512 - 3 * KROWS, 2 * HC), BF16)
    zright[6 * HR : 1280] = jnp.zeros((1280 - 6 * HR, 2 * HC), BF16)
    put_left(xo, lambda rows: coeffs[0, 0, rows], size)
    local[1].wait()
    own_part[...] = dot(xo[0:size], fo[...])
    local[0].wait()
    for r in range(0, size, 32):
        rows = slice(r, r + 32)
        planes = [dirty[n, 0, rows] for n in range(bands)]
        for i, t in enumerate(terms):
            total = planes[0] * weight(0, t)
            for n in range(1, bands):
                total += planes[n] * weight(n, t)
            dsum[i, rows] = total

    for copy in local[2:]:
        copy.wait()

    for i in range(2):
        x_copies[i].wait_recv()
        f_copies[i].start()

    a_copies[2].wait_recv()
    late_sum[...] = late[away_late + core] + late_a[...]
    x_copies[2].start()

    for d in NEIGHBOURS:
        dr, dc = d
        there = exists(d)
        incoming = halo((-dr, -dc))

        @pl.when(there)
        def _():
            incoming.wait_recv()

        if dr == 0:
            ref, i = side_in, (1 - dc) // 2
        elif dc == 0:
            ref, i = vert_in, (1 - dr) // 2
        else:
            ref, i = corner_in, (1 - dr) + (1 - dc) // 2

        @pl.when(jnp.logical_not(there))
        def _():
            ref[i] = jnp.zeros(ref.shape[1:], F32)

    def edge(right, left, m):
        top = jnp.where(m, right, left)
        bottom = pltpu.roll(jnp.where(m, left, right), LANES // 2, 1)
        return jnp.concatenate([top, bottom], axis=0)

    def place(ref, x, row, step):
        put_left(ref, lambda rows: x[rows], x.shape[0], row, step)

    place(xe, edge(side_in[0], side_in[1], half_mask((h, LANES))), 0, 64)
    small = half_mask((B // 2, LANES))
    for i in range(2):
        put_left(xo, lambda rows: vert_in[i, rows], B, size + i * B)
        place(xe, edge(corner_in[2 * i], corner_in[2 * i + 1], small), size + i * B, 64)
    total_rows = size + 2 * B
    acc[0:size] = own_part[...] + dot(xe[0:size], fe[...])
    acc[size:total_rows] = dot(xo[size:], fo[...]) + dot(xe[size:], fe[...])
    put_right(yr, lambda rows: acc[rows], total_rows, total_rows)
    acc[...] = dot(fr[...], yr[...])

    def halves(load, rows):
        below = slice(HR + rows.start, HR + rows.stop)
        cc, cs = load(rows, slice(0, HC)), load(rows, slice(HC, 2 * HC))
        sc, ss = load(below, slice(0, HC)), load(below, slice(HC, 2 * HC))
        return cc - ss, sc + cs, cc + ss, sc - cs

    for r in range(0, HR, 16):
        rows = slice(r, r + 16)
        for n, x in enumerate(halves(lambda a, b: acc[a, b], rows)):
            field[n, rows] = x

    def forwarded(i):
        other = early_x.at[piece(i, 1 - core)] if i < 2 else late_x.at[1 - core]
        pltpu.make_async_remote_copy(
            other, other, f_send.at[i], f_recv.at[i], device_id=sib
        ).wait_recv()

    blank = jnp.zeros((KROWS - SENT, 2 * LANES), F32)

    def kernels(first):
        turned = slice(TURNED, TURNED + 16)
        turned = early[turned] + early_b[turned] + early_x[turned]
        square = jnp.concatenate([turned[0:8], jnp.zeros((LANES - 8, LANES), F32)], axis=0)
        column = jnp.concatenate([jnp.transpose(square), turned[8:16]], axis=0)
        for i in range(2):
            s = g + terms[first + i]
            near = jnp.clip(s, 2, 4) if first else s
            rows = pl.ds(pl.multiple_of((near - 2) * SENT, 8), SENT)
            main = early[rows] + early_b[rows] + early_x[rows]
            if first:
                at = jnp.where(chip == 0, jnp.clip(s, 0, 1), jnp.clip(s, 5, 6) - 3)
                outer = late[at] + late_b[at] + late_x[at - 2 * chip]
                main = jnp.where(s == near, main, outer)
            own = jnp.where(lane == s, column, 0.0)
            block = jnp.concatenate([main, own], axis=1)
            place(pleft, jnp.concatenate([block, blank], axis=0), i * KROWS, 16)
        kacc[...] = dot(pleft[...], kc[...])
        for i in range(2):
            put_right(
                kright.at[i],
                lambda rows: kacc[i * KROWS + rows.start : i * KROWS + rows.stop],
                KROWS, KROWS,
            )
            kern[i] = dot(kr[...], kright[i])

    def term(i, put):
        for r in range(0, HR, 16):
            rows = slice(r, r + 16)
            a, b, c, d = (field[n, rows] for n in range(4))
            e, f, p, q = halves(lambda u, v: kern[i % 2, u, v], rows)
            re1, im1 = a * e - b * f, a * f + b * e
            re2, im2 = c * p - d * q, c * q + d * p
            parts = ((re1 + re2, im1 - im2), (im1 + im2, re2 - re1))
            for m in range(2):
                for n in range(2):
                    hi, lo = split(parts[m][n])
                    lanes = slice(n * HC, (n + 1) * HC)
                    at = m * HR + r
                    zright[at : at + 16, lanes] = hi
                    zright[2 * HR + at : 2 * HR + at + 16, lanes] = lo
                    zright[4 * HR + at : 4 * HR + at + 16, lanes] = hi
        acc[0:size] = dot(br[...], zright[...])
        put_left(wleft, lambda rows: acc[rows], size)
        for j in range(2):
            rows = slice(j * h, (j + 1) * h)
            put(j, rows, dsum[i, rows] - dot(wleft[rows], bc[...]))

    def pair_copy(i, j):
        n = 2 * i + j
        rows = pl.ds(j * h, h)
        return pltpu.make_async_remote_copy(
            part.at[i, rows], pair_in.at[i, rows], t_send.at[n], t_recv.at[n], device_id=sib
        )

    def cross_copy(j):
        rows = pl.ds(j * h, h)
        return pltpu.make_async_remote_copy(
            term_x.at[rows], term_in.at[rows], t_send.at[4 + j], t_recv.at[4 + j], device_id=far
        )

    pairs = [[pair_copy(i, j) for j in range(2)] for i in range(2)]
    crosses = [cross_copy(j) for j in range(2)]

    def to_pair(i):
        def put(j, rows, value):
            part[i, rows] = value
            pairs[i][j].start()

        return put

    def to_far(j, rows, value):
        pairs[0][j].wait_recv()
        term_x[rows] = value + pair_in[0, rows]
        crosses[j].start()

    def to_out(j, rows, value):
        pairs[1][j].wait_recv()
        out[0, 0, rows] = value + pair_in[1, rows]

    forwarded(0)
    forwarded(1)
    b_copies[0].wait_recv()
    kernels(0)
    x_copies[2].wait_recv()
    f_copies[2].start()
    term(0, to_pair(0))
    term(1, to_far)
    forwarded(2)
    b_copies[1].wait_recv()
    kernels(2)
    term(2, to_pair(1))
    term(3, to_out)
    for j in range(2):
        rows = slice(j * h, (j + 1) * h)
        crosses[j].wait_recv()
        got[0, 0, rows] = term_in[rows]

    for d in NEIGHBOURS:
        @pl.when(exists(d))
        def _():
            halo(d).wait_send()

    for copy in (*a_copies, *b_copies, *x_copies, *f_copies, *pairs[0], *pairs[1], *crosses):
        copy.wait_send()


def body(coeffs, dirty, psf, band_offset):
    size = coeffs.shape[-1]
    span = size + 2 * B
    bands = dirty.shape[0]
    psf = psf.transpose(0, 2, 1, 3)
    facets = lax.axis_size("facet")
    consts = tables(size, span, psf.shape[-1])
    vmem = pl.BlockSpec(memory_space=pltpu.VMEM)
    hbm = pl.BlockSpec(memory_space=pltpu.HBM)
    dma = lambda n: pltpu.SemaphoreType.DMA((n,))
    scratch = [pltpu.VMEM(c.shape, BF16) for c in consts]
    scratch += [
        pltpu.VMEM(coeffs.shape, F32),
        pltpu.VMEM(dirty.shape, F32),
        pltpu.VMEM(psf.shape, F32),
        pltpu.VMEM((2 * HR, 2 * HC), F32),
        pltpu.VMEM((2 * KROWS, 2 * HC), F32),
        dma(10),
        pltpu.VMEM((2 * SHARE, LANES), F32),
        pltpu.VMEM((SHARE, LANES), F32),
        pltpu.VMEM((2 * SHARE, LANES), F32),
        pltpu.VMEM((SHARE, LANES), F32),
        pltpu.VMEM((2 * SHARE, LANES), F32),
        pltpu.VMEM((4, SENT, LANES), F32),
        pltpu.VMEM((SENT, LANES), F32),
        pltpu.VMEM((4, SENT, LANES), F32),
        pltpu.VMEM((SENT, LANES), F32),
        pltpu.VMEM((2, SENT, LANES), F32),
        pltpu.VMEM((SENT, LANES), F32),
        pltpu.VMEM((2, size // 2, LANES), F32),
        pltpu.VMEM((2, size // 2, LANES), F32),
        pltpu.VMEM((4, B // 2, LANES), F32),
        pltpu.VMEM((4, B // 2, LANES), F32),
        pltpu.VMEM((2, B, size), F32),
        pltpu.VMEM((span, 3 * size), BF16),
        pltpu.VMEM((span, 3 * LANES), BF16),
        pltpu.VMEM((size, 2 * HC), F32),
        pltpu.VMEM((3 * span, 2 * HC), BF16),
        pltpu.VMEM((2 * KROWS, 6 * LANES), BF16),
        pltpu.VMEM((2, 512, 2 * HC), BF16),
        pltpu.VMEM((1280, 2 * HC), BF16),
        pltpu.VMEM((size, 6 * HC), BF16),
        pltpu.VMEM((4, HR, HC), F32),
        pltpu.VMEM((2, 2 * HR, 2 * HC), F32),
        pltpu.VMEM((TERMS, size, size), F32),
        pltpu.VMEM((2, size, size), F32),
        pltpu.VMEM((2, size, size), F32),
        pltpu.VMEM((size, size), F32),
        pltpu.VMEM((size, size), F32),
        dma(8), dma(8), dma(5), dma(5), dma(3), dma(3), dma(3), dma(3), dma(6), dma(6),
    ]

    def run(*args):
        kernel(facets, size, bands, *args)

    shape = jax.ShapeDtypeStruct(coeffs.shape, F32)
    kept, received = pl.pallas_call(
        run,
        out_shape=(shape, shape),
        in_specs=[hbm, hbm, hbm, pl.BlockSpec(memory_space=pltpu.SMEM)] + [hbm] * 7,
        out_specs=(vmem, vmem),
        scratch_shapes=scratch,
        compiler_params=pltpu.CompilerParams(
            collective_id=0, has_side_effects=True, vmem_limit_bytes=54592 * 1024
        ),
        cost_estimate=pl.CostEstimate(flops=4_000_000_000, bytes_accessed=8_000_000, transcendentals=0),
    )(coeffs, dirty, psf, band_offset, *[jnp.asarray(c) for c in consts])
    return kept + received


def solution(mesh):
    placed = (
        P("band", "facet", None, None),
        P("band", "facet", None, None),
        P("band", "facet", None, None),
        P("band"),
    )
    return jax.shard_map(
        body, mesh=mesh, in_specs=placed, out_specs=P("band", "facet", None, None), check_vma=False
    )
```

```python
import ml_dtypes
import numpy as np
import jax
import jax.numpy as jnp
from jax import lax
from jax.experimental import pallas as pl
from jax.experimental.pallas import tpu as pltpu
from jax.sharding import PartitionSpec as P

B = 64
TERMS = 4
FGY = 4
POWERS = 2 * TERMS - 1
EARLY = (2, 3, 4)
LATE = (0, 1, 5, 6)
HR = 208
HC = 256
KROWS = 144
SENT = 136
TURNED = 3 * SENT
SHARE = 216
PIECES = ((0, 112), (112, 104))
LANES = 128
F32 = jnp.float32
BF16 = jnp.bfloat16
NEIGHBOURS = [(dr, dc) for dr in (-1, 0, 1) for dc in (-1, 0, 1) if (dr, dc) != (0, 0)]


def forward_table(positions, length, half):
    k = np.arange(half)
    angle = 2 * np.pi * ((k[:, None] * positions[None, :]) % length) / length
    ok = (k <= length // 2)[:, None]
    return np.concatenate([np.cos(angle) * ok, np.sin(angle) * ok], axis=0)


def inverse_table(positions, length, half):
    k = np.arange(half)
    fold = np.where((k == 0) | (k == length // 2), 1.0, 2.0) / length
    return forward_table(positions, length, half) * np.concatenate([fold, fold])[:, None]


def split_table(table):
    hi = table.astype(np.float32).astype(ml_dtypes.bfloat16)
    lo = (table - hi.astype(np.float64)).astype(np.float32).astype(ml_dtypes.bfloat16)
    return hi, lo


def left_table(table, width):
    hi, lo = split_table(table)
    whole = np.concatenate([hi, hi, lo], axis=1)
    return np.pad(whole, ((0, 0), (0, width - whole.shape[1])))


def right_table(table):
    hi, lo = split_table(table)
    return np.concatenate([hi, lo, hi], axis=0)


def tables(size, span, k):
    pos = np.arange(span)
    out = np.arange(size)
    ker = np.arange(k) - B
    cols = forward_table(pos, span, HC).T
    field_own, field_edge = right_table(cols[:size]), right_table(cols[size:])
    field_rows = left_table(forward_table(pos, span, HR), 3 * span)
    kern = forward_table(ker, span, HC).T
    kern = np.concatenate([kern[:LANES], np.repeat(kern[LANES:], LANES, axis=0)], axis=0)
    kern_cols = right_table(kern)
    rows = np.pad(forward_table(ker, span, HR), ((0, 0), (0, KROWS - k)))
    kern_rows = left_table(rows, 512)
    back_rows = left_table(inverse_table(out, span, HR).T / 2, 1280)
    back_cols = right_table(inverse_table(out, span, HC))
    return field_own, field_edge, field_rows, kern_cols, kern_rows, back_rows, back_cols


def split(x):
    hi = x.astype(BF16)
    return hi, (x - hi.astype(F32)).astype(BF16)


def put_left(ref, load, height, row=0, step=16):
    for r in range(0, height, step):
        x = load(slice(r, r + step))
        hi, lo = split(x)
        w = x.shape[1]
        rows = slice(row + r, row + r + step)
        ref[rows, 0:w] = hi
        ref[rows, w : 2 * w] = hi
        ref[rows, 2 * w : 3 * w] = lo


def put_right(ref, load, height, pitch, step=16):
    for r in range(0, height, step):
        hi, lo = split(load(slice(r, r + step)))
        ref[r : r + step] = hi
        ref[pitch + r : pitch + r + step] = lo
        ref[2 * pitch + r : 2 * pitch + r + step] = hi


def dot(a, b):
    return jnp.dot(a, b, preferred_element_type=F32)


def half_mask(shape):
    return lax.broadcasted_iota(jnp.int32, shape, 1) < LANES // 2


def pack(first, second, left):
    mask = half_mask(first.shape)
    moved = pltpu.roll(second, LANES // 2, 1)
    return jnp.where(mask, first, moved) if left else jnp.where(mask, moved, first)


def kernel(
    facets, size, bands,
    coeffs_hbm, dirty_hbm, psf_hbm, offset, *refs,
):
    tables_hbm = refs[:7]
    out, got = refs[7:9]
    (fo, fe, fr, kc, kr, br, bc, coeffs, dirty, psf, acc, kacc, local_sem,
     early, early_a, early_b, early_sum, early_x, late, late_a, late_b, late_sum, late_x, last,
     side, side_in, corner, corner_in, vert_in,
     xo, xe, own_part, yr, pleft, kright, zright, wleft, field, kern, dsum, part, pair_in, term_x,
     term_in, halo_send, halo_recv, s_send, s_recv, x_send, x_recv, f_send, f_recv,
     t_send, t_recv) = refs[9:]
    vm = (fo, fe, fr, kc, kr, br, bc)

    g = lax.axis_index("band")
    facet = lax.axis_index("facet")
    chip, core = g // 2, g % 2
    sib = {"band": 2 * chip + 1 - core}
    far = {"band": 2 * (1 - chip) + core}
    q = (facet + FGY + FGY // 2) % facets
    row, col = q // FGY, q % FGY

    def exists(d):
        r, c = row + d[0], col + d[1]
        return (r >= 0) & (r < facets // FGY) & (c >= 0) & (c < FGY)

    def device(d):
        return {"facet": (facet + FGY * d[0] + d[1] + facets) % facets}

    inputs = [
        pltpu.make_async_copy(psf_hbm, psf, local_sem.at[8]),
        pltpu.make_async_copy(coeffs_hbm, coeffs, local_sem.at[9]),
    ]
    for copy in inputs:
        copy.start()

    barrier = pltpu.get_barrier_semaphore()
    count = 2
    for d in NEIGHBOURS:
        there = exists(d)
        count = count + there.astype(jnp.int32)

        @pl.when(there)
        def _():
            pl.semaphore_signal(barrier, inc=1, device_id=device(d))

    for peer in (sib, far):
        pl.semaphore_signal(barrier, inc=1, device_id=peer)

    local = [pltpu.make_async_copy(dirty_hbm, dirty, local_sem.at[7])]
    local += [pltpu.make_async_copy(tables_hbm[i], vm[i], local_sem.at[i]) for i in range(7)]
    for copy in local:
        copy.start()

    powers = []
    for b in range(bands):
        w = offset[b]
        row_b = [jnp.float32(1.0)]
        for _ in range(1, POWERS):
            row_b.append(row_b[-1] * w)
        powers.append(row_b)

    k = psf.shape[1]
    lane = lax.broadcasted_iota(jnp.int32, (1, LANES), 1)
    tail = jnp.zeros((SENT - LANES, LANES), F32)
    for i in range(3):
        early[i * SENT + LANES : (i + 1) * SENT] = tail
    early[TURNED + 16 :] = jnp.zeros((2 * SHARE - TURNED - 16, LANES), F32)
    for i in range(4):
        late[i, LANES:SENT] = tail
    last[LANES:SENT] = tail
    w_rows = []
    for b in range(bands):
        w_row = jnp.zeros((1, LANES), F32)
        for s in range(POWERS):
            w_row = jnp.where(lane == s, powers[b][s], w_row)
        w_rows.append(w_row)
    def combine(wanted, with_last):
        for top in range(0, k, 32):
            rows = slice(top, min(top + 32, k))
            planes = [psf[b, rows, 0, 0:LANES] for b in range(bands)]
            for s in wanted:
                total = planes[0]
                if s:
                    total = total * powers[0][s]
                for b in range(1, bands):
                    total += planes[b] * powers[b][s]
                if s in EARLY:
                    at = EARLY.index(s) * SENT
                    early[at + rows.start : at + rows.stop] = total
                else:
                    late[LATE.index(s), rows] = total
            if with_last:
                total = psf[0, rows, 0, LANES:k] * w_rows[0]
                for b in range(1, bands):
                    total += psf[b, rows, 0, LANES:k] * w_rows[b]
                last[rows] = total

    h = size // 2
    inputs[1].wait()
    side[0] = pack(coeffs[0, 0, 0:h, 0:LANES], coeffs[0, 0, h:size, 0:LANES], True)
    side[1] = pack(
        coeffs[0, 0, 0:h, size - LANES : size], coeffs[0, 0, h:size, size - LANES : size], False
    )
    for i, top in enumerate((0, size - B)):
        for j in range(2):
            lanes = slice(0, LANES) if j == 0 else slice(size - LANES, size)
            corner[2 * i + j] = pack(
                coeffs[0, 0, top : top + B // 2, lanes],
                coeffs[0, 0, top + B // 2 : top + B, lanes],
                j == 0,
            )

    def halo(d):
        dr, dc = d
        if dr == 0:
            i = (dc + 1) // 2
            src, dst = side.at[i], side_in.at[i]
        elif dc == 0:
            i = (dr + 1) // 2
            src = coeffs.at[0, 0, pl.ds(i * (size - B), B), :]
            dst = vert_in.at[i]
        else:
            i = (dr + 1) + (dc + 1) // 2
            src, dst = corner.at[i], corner_in.at[i]
        n = NEIGHBOURS.index(d)
        return pltpu.make_async_remote_copy(
            src, dst, halo_send.at[n], halo_recv.at[n], device_id=device(d)
        )

    inputs[0].wait()
    combine(EARLY, True)
    early[TURNED : TURNED + 8] = jnp.transpose(last[0:LANES])[0:8]
    early[TURNED + 8 : TURNED + 16] = last[LANES:SENT]
    pl.semaphore_wait(barrier, count)

    def to_sib(src, dst, i):
        return pltpu.make_async_remote_copy(src, dst, s_send.at[i], s_recv.at[i], device_id=sib)

    away_late = jnp.where(chip == 0, 2, 0)

    def piece(i, who):
        at, rows = PIECES[i]
        return pl.ds(pl.multiple_of(SHARE * who + at, 8), rows)

    a_copies = [to_sib(early.at[piece(i, 1 - core)], early_a.at[piece(i, 0)], i) for i in range(2)]
    a_copies.append(to_sib(late.at[away_late + 1 - core], late_a, 2))
    b_copies = [to_sib(early, early_b, 3), to_sib(late, late_b, 4)]
    for d in sorted(NEIGHBOURS, key=lambda d: abs(d[0]) + abs(d[1]) == 2):
        @pl.when(exists(d))
        def _():
            halo(d).start()

    a_copies[0].start()
    a_copies[1].start()

    x_copies, f_copies = [], []
    for i in range(3):
        src, slot = late_sum, late_x.at[core]
        if i < 2:
            src, slot = early_sum.at[piece(i, 0)], early_x.at[piece(i, core)]
        x_copies.append(
            pltpu.make_async_remote_copy(src, slot, x_send.at[i], x_recv.at[i], device_id=far)
        )
        f_copies.append(
            pltpu.make_async_remote_copy(slot, slot, f_send.at[i], f_recv.at[i], device_id=sib)
        )
    for i in range(2):
        a_copies[i].wait_recv()
        early_sum[piece(i, 0)] = early[piece(i, core)] + early_a[piece(i, 0)]
        x_copies[i].start()
    combine(LATE, False)
    a_copies[2].start()
    b_copies[0].start()
    b_copies[1].start()

    away, home = 2 * (1 - chip), 2 * chip
    terms = (away + 1 - core, away + core, home + 1 - core, home + core)

    def weight(b, t):
        w = powers[b]
        return jnp.where(t == 0, w[0], jnp.where(t == 1, w[1], jnp.where(t == 2, w[2], w[3])))

    kright[:, 3 * KROWS : 512] = jnp.zeros((2, 512 - 3 * KROWS, 2 * HC), BF16)
    zright[6 * HR : 1280] = jnp.zeros((1280 - 6 * HR, 2 * HC), BF16)
    put_left(xo, lambda rows: coeffs[0, 0, rows], size)
    local[1].wait()
    own_part[...] = dot(xo[0:size], fo[...])
    local[0].wait()
    for r in range(0, size, 32):
        rows = slice(r, r + 32)
        planes = [dirty[n, 0, rows] for n in range(bands)]
        for i, t in enumerate(terms):
            total = planes[0] * weight(0, t)
            for n in range(1, bands):
                total += planes[n] * weight(n, t)
            dsum[i, rows] = total

    for copy in local[2:]:
        copy.wait()

    for i in range(2):
        x_copies[i].wait_recv()
        f_copies[i].start()

    a_copies[2].wait_recv()
    late_sum[...] = late[away_late + core] + late_a[...]
    x_copies[2].start()

    def place(ref, x, row, step):
        put_left(ref, lambda rows: x[rows], x.shape[0], row, step)

    def forwarded(i):
        other = early_x.at[piece(i, 1 - core)] if i < 2 else late_x.at[1 - core]
        pltpu.make_async_remote_copy(
            other, other, f_send.at[i], f_recv.at[i], device_id=sib
        ).wait_recv()

    blank = jnp.zeros((KROWS - SENT, 2 * LANES), F32)

    def kernels(first):
        turned = slice(TURNED, TURNED + 16)
        turned = early[turned] + early_b[turned] + early_x[turned]
        square = jnp.concatenate([turned[0:8], jnp.zeros((LANES - 8, LANES), F32)], axis=0)
        column = jnp.concatenate([jnp.transpose(square), turned[8:16]], axis=0)
        for i in range(2):
            s = g + terms[first + i]
            near = jnp.clip(s, 2, 4) if first else s
            rows = pl.ds(pl.multiple_of((near - 2) * SENT, 8), SENT)
            main = early[rows] + early_b[rows] + early_x[rows]
            if first:
                at = jnp.where(chip == 0, jnp.clip(s, 0, 1), jnp.clip(s, 5, 6) - 3)
                outer = late[at] + late_b[at] + late_x[at - 2 * chip]
                main = jnp.where(s == near, main, outer)
            own = jnp.where(lane == s, column, 0.0)
            block = jnp.concatenate([main, own], axis=1)
            place(pleft, jnp.concatenate([block, blank], axis=0), i * KROWS, 16)
        kacc[...] = dot(pleft[...], kc[...])
        for i in range(2):
            put_right(
                kright.at[i],
                lambda rows: kacc[i * KROWS + rows.start : i * KROWS + rows.stop],
                KROWS, KROWS,
            )
            kern[i] = dot(kr[...], kright[i])

    forwarded(0)
    forwarded(1)
    b_copies[0].wait_recv()
    kernels(0)

    for d in NEIGHBOURS:
        dr, dc = d
        there = exists(d)
        incoming = halo((-dr, -dc))

        @pl.when(there)
        def _():
            incoming.wait_recv()

        if dr == 0:
            ref, i = side_in, (1 - dc) // 2
        elif dc == 0:
            ref, i = vert_in, (1 - dr) // 2
        else:
            ref, i = corner_in, (1 - dr) + (1 - dc) // 2

        @pl.when(jnp.logical_not(there))
        def _():
            ref[i] = jnp.zeros(ref.shape[1:], F32)

    def edge(right, left, m):
        top = jnp.where(m, right, left)
        bottom = pltpu.roll(jnp.where(m, left, right), LANES // 2, 1)
        return jnp.concatenate([top, bottom], axis=0)

    place(xe, edge(side_in[0], side_in[1], half_mask((h, LANES))), 0, 64)
    small = half_mask((B // 2, LANES))
    for i in range(2):
        put_left(xo, lambda rows: vert_in[i, rows], B, size + i * B)
        place(xe, edge(corner_in[2 * i], corner_in[2 * i + 1], small), size + i * B, 64)
    total_rows = size + 2 * B
    acc[0:size] = own_part[...] + dot(xe[0:size], fe[...])
    acc[size:total_rows] = dot(xo[size:], fo[...]) + dot(xe[size:], fe[...])
    put_right(yr, lambda rows: acc[rows], total_rows, total_rows)
    acc[...] = dot(fr[...], yr[...])

    def halves(load, rows):
        below = slice(HR + rows.start, HR + rows.stop)
        cc, cs = load(rows, slice(0, HC)), load(rows, slice(HC, 2 * HC))
        sc, ss = load(below, slice(0, HC)), load(below, slice(HC, 2 * HC))
        return cc - ss, sc + cs, cc + ss, sc - cs

    for r in range(0, HR, 16):
        rows = slice(r, r + 16)
        for n, x in enumerate(halves(lambda a, b: acc[a, b], rows)):
            field[n, rows] = x

    def term(i, put):
        for r in range(0, HR, 16):
            rows = slice(r, r + 16)
            a, b, c, d = (field[n, rows] for n in range(4))
            e, f, p, q = halves(lambda u, v: kern[i % 2, u, v], rows)
            re1, im1 = a * e - b * f, a * f + b * e
            re2, im2 = c * p - d * q, c * q + d * p
            parts = ((re1 + re2, im1 - im2), (im1 + im2, re2 - re1))
            for m in range(2):
                for n in range(2):
                    hi, lo = split(parts[m][n])
                    lanes = slice(n * HC, (n + 1) * HC)
                    at = m * HR + r
                    zright[at : at + 16, lanes] = hi
                    zright[2 * HR + at : 2 * HR + at + 16, lanes] = lo
                    zright[4 * HR + at : 4 * HR + at + 16, lanes] = hi
        acc[0:size] = dot(br[...], zright[...])
        put_left(wleft, lambda rows: acc[rows], size)
        for j in range(2):
            rows = slice(j * h, (j + 1) * h)
            put(j, rows, dsum[i, rows] - dot(wleft[rows], bc[...]))

    def pair_copy(i, j):
        n = 2 * i + j
        rows = pl.ds(j * h, h)
        return pltpu.make_async_remote_copy(
            part.at[i, rows], pair_in.at[i, rows], t_send.at[n], t_recv.at[n], device_id=sib
        )

    def cross_copy(j):
        rows = pl.ds(j * h, h)
        return pltpu.make_async_remote_copy(
            term_x.at[rows], term_in.at[rows], t_send.at[4 + j], t_recv.at[4 + j], device_id=far
        )

    pairs = [[pair_copy(i, j) for j in range(2)] for i in range(2)]
    crosses = [cross_copy(j) for j in range(2)]

    def to_pair(i):
        def put(j, rows, value):
            part[i, rows] = value
            pairs[i][j].start()

        return put

    def to_far(j, rows, value):
        pairs[0][j].wait_recv()
        term_x[rows] = value + pair_in[0, rows]
        crosses[j].start()

    def to_out(j, rows, value):
        pairs[1][j].wait_recv()
        out[0, 0, rows] = value + pair_in[1, rows]

    x_copies[2].wait_recv()
    f_copies[2].start()
    term(0, to_pair(0))
    term(1, to_far)
    forwarded(2)
    b_copies[1].wait_recv()
    kernels(2)
    term(2, to_pair(1))
    term(3, to_out)
    for j in range(2):
        rows = slice(j * h, (j + 1) * h)
        crosses[j].wait_recv()
        got[0, 0, rows] = term_in[rows]

    for d in NEIGHBOURS:
        @pl.when(exists(d))
        def _():
            halo(d).wait_send()

    for copy in (*a_copies, *b_copies, *x_copies, *f_copies, *pairs[0], *pairs[1], *crosses):
        copy.wait_send()


def body(coeffs, dirty, psf, band_offset):
    size = coeffs.shape[-1]
    span = size + 2 * B
    bands = dirty.shape[0]
    psf = psf.transpose(0, 2, 1, 3)
    facets = lax.axis_size("facet")
    consts = tables(size, span, psf.shape[-1])
    vmem = pl.BlockSpec(memory_space=pltpu.VMEM)
    hbm = pl.BlockSpec(memory_space=pltpu.HBM)
    dma = lambda n: pltpu.SemaphoreType.DMA((n,))
    scratch = [pltpu.VMEM(c.shape, BF16) for c in consts]
    scratch += [
        pltpu.VMEM(coeffs.shape, F32),
        pltpu.VMEM(dirty.shape, F32),
        pltpu.VMEM(psf.shape, F32),
        pltpu.VMEM((2 * HR, 2 * HC), F32),
        pltpu.VMEM((2 * KROWS, 2 * HC), F32),
        dma(10),
        pltpu.VMEM((2 * SHARE, LANES), F32),
        pltpu.VMEM((SHARE, LANES), F32),
        pltpu.VMEM((2 * SHARE, LANES), F32),
        pltpu.VMEM((SHARE, LANES), F32),
        pltpu.VMEM((2 * SHARE, LANES), F32),
        pltpu.VMEM((4, SENT, LANES), F32),
        pltpu.VMEM((SENT, LANES), F32),
        pltpu.VMEM((4, SENT, LANES), F32),
        pltpu.VMEM((SENT, LANES), F32),
        pltpu.VMEM((2, SENT, LANES), F32),
        pltpu.VMEM((SENT, LANES), F32),
        pltpu.VMEM((2, size // 2, LANES), F32),
        pltpu.VMEM((2, size // 2, LANES), F32),
        pltpu.VMEM((4, B // 2, LANES), F32),
        pltpu.VMEM((4, B // 2, LANES), F32),
        pltpu.VMEM((2, B, size), F32),
        pltpu.VMEM((span, 3 * size), BF16),
        pltpu.VMEM((span, 3 * LANES), BF16),
        pltpu.VMEM((size, 2 * HC), F32),
        pltpu.VMEM((3 * span, 2 * HC), BF16),
        pltpu.VMEM((2 * KROWS, 6 * LANES), BF16),
        pltpu.VMEM((2, 512, 2 * HC), BF16),
        pltpu.VMEM((1280, 2 * HC), BF16),
        pltpu.VMEM((size, 6 * HC), BF16),
        pltpu.VMEM((4, HR, HC), F32),
        pltpu.VMEM((2, 2 * HR, 2 * HC), F32),
        pltpu.VMEM((TERMS, size, size), F32),
        pltpu.VMEM((2, size, size), F32),
        pltpu.VMEM((2, size, size), F32),
        pltpu.VMEM((size, size), F32),
        pltpu.VMEM((size, size), F32),
        dma(8), dma(8), dma(5), dma(5), dma(3), dma(3), dma(3), dma(3), dma(6), dma(6),
    ]

    def run(*args):
        kernel(facets, size, bands, *args)

    shape = jax.ShapeDtypeStruct(coeffs.shape, F32)
    kept, received = pl.pallas_call(
        run,
        out_shape=(shape, shape),
        in_specs=[hbm, hbm, hbm, pl.BlockSpec(memory_space=pltpu.SMEM)] + [hbm] * 7,
        out_specs=(vmem, vmem),
        scratch_shapes=scratch,
        compiler_params=pltpu.CompilerParams(
            collective_id=0, has_side_effects=True, vmem_limit_bytes=54592 * 1024
        ),
        cost_estimate=pl.CostEstimate(flops=4_000_000_000, bytes_accessed=8_000_000, transcendentals=0),
    )(coeffs, dirty, psf, band_offset, *[jnp.asarray(c) for c in consts])
    return kept + received


def solution(mesh):
    placed = (
        P("band", "facet", None, None),
        P("band", "facet", None, None),
        P("band", "facet", None, None),
        P("band"),
    )
    return jax.shard_map(
        body, mesh=mesh, in_specs=placed, out_specs=P("band", "facet", None, None), check_vma=False
    )
```
